128 devices in a mesh: dp: 64 (over x, y_lo, z, core), ctx: 2 (over y_hi).
Axes of the slice: x: 4, y: 4 (y_hi: 2, y_lo: 2; y = y_hi * 2 + y_lo), z: 4, core: 2. Of those that a mesh axis runs over, the one named last changes fastest.
Arguments:
- tokens: bfloat16 [16384, 896], P(('dp', 'ctx')), may hold values from -6 to 6
- segments: int32 [16384], P(('dp', 'ctx')), may hold values from 0 to 1, as said below
- gain_attn: bfloat16 [896], P(('dp', 'ctx')), may hold values from 0.5 to 1.5
- w_query: bfloat16 [896, 896], P(('dp', 'ctx')), may hold values from -0.1875 to 0.1875
- w_key: bfloat16 [896, 128], P(('dp', 'ctx')), may hold values from -0.1875 to 0.1875
- w_value: bfloat16 [896, 128], P(('dp', 'ctx')), may hold values from -0.1875 to 0.1875
- bias_qkv: bfloat16 [1152], P(('dp', 'ctx')), may hold values from -3 to 3
- w_out: bfloat16 [896, 896], P(('dp', 'ctx')), may hold values from -0.75 to 0.75
- gain_ffn: bfloat16 [896], P(('dp', 'ctx')), may hold values from 0.5 to 1.5
- w_gate: bfloat16 [896, 4864], P(('dp', 'ctx')), may hold values from -0.1875 to 0.1875
- w_up: bfloat16 [896, 4864], P(('dp', 'ctx')), may hold values from -0.1875 to 0.1875
- w_down: bfloat16 [4864, 896], P(('dp', 'ctx')), may hold values from -0.078125 to 0.078125
- cotangent: bfloat16 [16384, 896], P(('dp', 'ctx')), may hold values from -6 to 6
Outputs:
- output: bfloat16 [16384, 896], P(('dp', 'ctx'))
- input_grad: bfloat16 [16384, 896], P(('dp', 'ctx'))
- grad_gain_attn: float32 [896], P(('dp', 'ctx'))
- grad_w_query: float32 [896, 896], P(('dp', 'ctx'))
- grad_w_key: float32 [896, 128], P(('dp', 'ctx'))
- grad_w_value: float32 [896, 128], P(('dp', 'ctx'))
- grad_bias_qkv: float32 [1152], P(('dp', 'ctx'))
- grad_w_out: float32 [896, 896], P(('dp', 'ctx'))
- grad_gain_ffn: float32 [896], P(('dp', 'ctx'))
- grad_w_gate: float32 [896, 4864], P(('dp', 'ctx'))
- grad_w_up: float32 [896, 4864], P(('dp', 'ctx'))
- grad_w_down: float32 [4864, 896], P(('dp', 'ctx'))
The draws below stay inside these ranges and needn't reach their ends.
Inputs may be any that keep to these rules, and one draw needn't show every extreme that they name: `segments`: in each sequence of 256 consecutive tokens the numbers are 0, then 1, each in one non-empty run; the run of 1 begins at an index from 32 to 224.
All inputs are finite; a program needn't handle non-finite values.
Results may differ from the reference program's by a relative error of at most 0.017.
Values may be sent and summed in bfloat16 or wider, within the bound.
A program may use at most 192 MiB of HBM per device.

```python
import jax
import jax.numpy as jnp
from jax import lax

D = 896
HEADS = 14
KV_HEADS = 2
HEAD = 64
FF = 4864
SEQ = 256
TOKENS = 16384


def draw_segments(key, part):
    key = jax.random.fold_in(key, 7)
    seq_count = TOKENS // SEQ
    margin = max(1, SEQ // 8)
    cut = jax.random.randint(key, (seq_count, 1), margin, SEQ - margin + 1)
    places = jnp.arange(SEQ, dtype=jnp.int32)[None, :]
    numbers = (places >= cut).astype(jnp.int32)
    return numbers.reshape(TOKENS)


def block_scale(stream_key, shape, cuts, low, top_value):
    loudness = 1.0
    for position, parts in cuts:
        steps = jax.random.uniform(jax.random.fold_in(jax.random.fold_in(stream_key, 6), position), (parts,), jnp.float32, low / len(cuts), top_value / len(cuts))
        loudness = loudness * jnp.repeat(jnp.exp(steps), shape[position] // parts).reshape((-1,) + (1,) * (len(shape) - 1 - position))
    return loudness


def noise(rng, shape, scale, reach, split=(), kind=jnp.bfloat16):
    array = scale * jax.random.normal(rng, shape, jnp.float32)
    if split:
        array = array * block_scale(rng, shape, split, -0.22, 0.18)
    return jnp.clip(array, -reach, reach).astype(kind)


def setup_inputs(seed: int = 0) -> dict:
    key_list = jax.random.split(jax.random.key(seed), 14)
    return {
        "tokens": noise(key_list[0], (TOKENS, D), 1.0, 6.0, ((0, 128),)),
        "segments": draw_segments(jax.random.fold_in(key_list[13], 71), 0),
        "gain_attn": jnp.clip(1.0 + 0.1 * jax.random.normal(key_list[2], (D,), jnp.float32), 0.5, 1.5).astype(jnp.bfloat16),
        "w_query": noise(key_list[3], (D, D), D ** -0.5, 0.1875, ((0, 128),)),
        "w_key": noise(key_list[4], (D, KV_HEADS * HEAD), D ** -0.5, 0.1875, ((0, 128),)),
        "w_value": noise(key_list[5], (D, KV_HEADS * HEAD), D ** -0.5, 0.1875, ((0, 128),)),
        "bias_qkv": noise(key_list[6], (D + 2 * KV_HEADS * HEAD,), 0.5, 3.0, ((0, 128),)),
        "w_out": noise(key_list[7], (D, D), (D // 16) ** -0.5, 0.75, ((0, 128),)),
        "gain_ffn": jnp.clip(1.0 + 0.1 * jax.random.normal(key_list[8], (D,), jnp.float32), 0.5, 1.5).astype(jnp.bfloat16),
        "w_gate": noise(key_list[9], (D, FF), D ** -0.5, 0.1875, ((0, 128),)),
        "w_up": noise(key_list[10], (D, FF), D ** -0.5, 0.1875, ((0, 128),)),
        "w_down": noise(key_list[11], (FF, D), FF ** -0.5, 0.078125, ((0, 128),)),
        "cotangent": noise(key_list[12], (TOKENS, D), 1.0, 6.0, ((0, 128),)),
    }


epsilon = 1e-06
masked_value = -1000000000.0
rope_base = 1000000.0
highest = lax.Precision.HIGHEST

@jax.custom_vjp
def low(v):
    return lax.optimization_barrier(v.astype(jnp.bfloat16)).astype(jnp.float32)

@jax.custom_vjp
def low_back(v):
    return v

def low_keep(v):
    return (low(v), None)

def low_pass(kept, grad):
    return (grad,)

def back_keep(v):
    return (v, None)

def back_low(kept, grad):
    return (low(grad),)
low.defvjp(low_keep, low_pass)
low_back.defvjp(back_keep, back_low)

def project(values, weight_matrix):
    return jnp.einsum('bld,dx->blx', values, weight_matrix, precision=highest)

def rotary_tables(places):
    half_width = HEAD // 2
    frequency = rope_base ** (-2.0 * jnp.arange(half_width, dtype=jnp.float32) / HEAD)
    angles = places.astype(jnp.float32)[:, :, None] * frequency[None, None, :]
    return (jnp.cos(angles)[:, :, None, :], jnp.sin(angles)[:, :, None, :])

def rotate(values, cosine, sine_part):
    half_width = values.shape[-1] // 2
    front_half = values[..., :half_width]
    back_half = values[..., half_width:]
    return jnp.concatenate([front_half * cosine - back_half * sine_part, back_half * cosine + front_half * sine_part], axis=-1)

def layer(inputs, segment_ids, gain_attn, w_query, w_key, w_value, bias_qkv, w_out, gain_ffn, w_gate, w_up, w_down):
    batch_size, seq_length, width = inputs.shape
    group_width = HEADS // KV_HEADS
    kv_width = KV_HEADS * HEAD
    bias_query = bias_qkv[:width]
    bias_key = bias_qkv[width:width + kv_width]
    bias_value = bias_qkv[width + kv_width:]
    places = jnp.arange(seq_length, dtype=jnp.int32)
    before = lax.optimization_barrier(jnp.sum((segment_ids[:, None, :] < segment_ids[:, :, None]).astype(jnp.int32), axis=-1))
    cosine, sine_part = rotary_tables(places[None, :] - before)
    allowed = (segment_ids[:, :, None] == segment_ids[:, None, :]) & (places[:, None] >= places[None, :])[None]
    inverse_attn = lax.rsqrt(lax.optimization_barrier(jnp.mean(inputs * inputs, axis=-1, keepdims=True)) + epsilon)
    normed = low(inputs * inverse_attn * gain_attn)
    query_rows = low(rotate(low_back(project(normed, w_query) + bias_query).reshape(batch_size, seq_length, HEADS, HEAD), cosine, sine_part))
    key_rows = low(rotate(low_back(project(normed, w_key) + bias_key).reshape(batch_size, seq_length, KV_HEADS, HEAD), cosine, sine_part))
    value_rows = low_back(low(project(normed, w_value) + bias_value)).reshape(batch_size, seq_length, KV_HEADS, HEAD)
    query_grouped = query_rows.reshape(batch_size, seq_length, KV_HEADS, group_width, HEAD)
    raw_scores = low_back(jnp.einsum('bqkgd,blkd->bkgql', query_grouped, key_rows, precision=highest))
    logits = jnp.where(allowed[:, None, None], raw_scores * HEAD ** (-0.5), masked_value)
    shifted = logits - lax.optimization_barrier(jnp.max(logits, axis=-1, keepdims=True))
    weights_raw = jnp.exp(shifted)
    attention_probs = weights_raw / lax.optimization_barrier(jnp.sum(weights_raw, axis=-1, keepdims=True))
    mixed = low_back(low(jnp.einsum('bkgql,blkd->bqkgd', low(attention_probs), value_rows, precision=highest)))
    attention_out = low_back(project(mixed.reshape(batch_size, seq_length, width), w_out))
    hidden = inputs + attention_out
    inverse_ffn = lax.rsqrt(lax.optimization_barrier(jnp.mean(hidden * hidden, axis=-1, keepdims=True)) + epsilon)
    normed_ffn = low(hidden * inverse_ffn * gain_ffn)
    gate_rows = low_back(project(normed_ffn, w_gate))
    up_rows = low_back(project(normed_ffn, w_up))
    product = low(gate_rows * jax.nn.sigmoid(gate_rows) * up_rows)
    return hidden + project(product, w_down)

def reference(tokens, segments, gain_attn, w_query, w_key, w_value, bias_qkv, w_out, gain_ffn, w_gate, w_up, w_down, cotangent):
    seq_count = TOKENS // SEQ
    group_size = max(1, 4096 // SEQ)
    while seq_count % group_size:
        group_size = group_size - 1
    step_count = seq_count // group_size

    def blocks(values):
        return values.reshape((step_count, group_size, SEQ) + values.shape[1:])
    weights = tuple((weight_item.astype(jnp.float32) for weight_item in (gain_attn, w_query, w_key, w_value, bias_qkv, w_out, gain_ffn, w_gate, w_up, w_down)))

    def step(totals, pieces):
        block_tokens, block_ids, block_cot = pieces

        def forward(inputs, *params):
            return layer(inputs, block_ids, *params)
        result, pull = jax.vjp(forward, block_tokens.astype(jnp.float32), *weights)
        grads = pull(block_cot.astype(jnp.float32))
        totals = tuple((total_part + new_part for total_part, new_part in zip(totals, grads[1:])))
        return (totals, (result.astype(jnp.bfloat16), grads[0].astype(jnp.bfloat16)))
    initial = tuple((jnp.zeros_like(weight_item) for weight_item in weights))
    totals, outcome = lax.scan(step, initial, (blocks(tokens), blocks(segments), blocks(cotangent)))
    outputs, input_grads = outcome
    return (outputs.reshape(TOKENS, D), input_grads.reshape(TOKENS, D), totals[0], totals[1], totals[2], totals[3], totals[4], totals[5], totals[6], totals[7], totals[8], totals[9])
```

```python
import functools

import jax
import jax.numpy as jnp
import numpy as np
from jax import lax
from jax.experimental import pallas as pl
from jax.experimental.pallas import tpu as pltpu
from jax.sharding import PartitionSpec as P

F32 = jnp.float32
BF16 = jnp.bfloat16
MESH = pl.DeviceIdType.MESH
D = 896
DP = 1024
FF = 4864
FS = 640
T = 128
VEC = 2 * D + 1152
EPS = 1e-6
MASKED = -1e9
ORDERS = (("x", "z", "y"), ("z", "x", "y"), ("y", "x", "z"), ("y", "z", "x"))


def iota(shape, axis):
    return lax.broadcasted_iota(jnp.int32, shape, axis)


def sevenths(v):
    return lax.shift_right_logical(v * 9363, 16)


def ninths(v):
    return lax.shift_right_logical(v * 7282, 16)


def slot_of(i):
    return (i >> 5) * 32 + ((i >> 2) & 3) * 8 + (i & 1) * 4 + ((i >> 4) & 1) * 2 + ((i >> 1) & 1)


def one_hot(test):
    return jnp.where(test, 1.0, 0.0).astype(BF16)


def mm(a, b):
    return jnp.dot(a, b, preferred_element_type=F32)


def mm_nt(a, b):
    return lax.dot_general(a, b, (((1,), (1,)), ((), ())), preferred_element_type=F32)


def mm_tn(a, b):
    return lax.dot_general(a, b, (((0,), (0,)), ((), ())), preferred_element_type=F32)


def split(v):
    hi = v.astype(BF16)
    return hi, (v - hi.astype(F32)).astype(BF16)


SCRATCH = dict(
    pkf=((8, 2048), F32),
    pk=((4, 16, 256), BF16),
    pkr=((4, 16, 256), BF16),
    aw=((8, 4, 4, 4, 16, 256), BF16),
    guf=((2, 8, 8, FS), F32),
    gus=((8, 16, FS), BF16),
    gui=((8, 16, FS), BF16),
    wg=((4, 4, 64, FS), BF16),
    wu=((4, 4, 64, FS), BF16),
    da=((4, 4, 40, 512), BF16),
    db=((4, 4, 40, 384), BF16),
    pad=((D, DP), BF16),
    order=((FS, FS), BF16),
    pick=((32, VEC), BF16),
    mask=((128, VEC), BF16),
    wdf=((40, D), F32),
    segs=((2, 8, 128), jnp.int32),
    kv=((2, T, 256), BF16),
    prob=((14, T, 256), F32),
    ball=((4, 2, T, DP), BF16),
    yall=((4, 2, T, D), BF16),
    mb=((4, 2 * T, FS), BF16),
    dgb=((4, 2 * T, FS), BF16),
    dub=((4, 2 * T, FS), BF16),
    po=((4, 2, T, D), BF16),
    pd=((4, 2, T, DP), BF16),
    qo=((4, T, D), BF16),
    qd=((4, T, DP), BF16),
    ro=((3, T, D), BF16),
    rd=((3, T, DP), BF16),
    gg=((4, 4, 64, FS), BF16),
    gu=((4, 4, 64, FS), BF16),
    ga=((4, 4, 40, 512), BF16),
    gb=((4, 4, 40, 384), BF16),
    rg1=((3, 4, 64, FS), BF16),
    ru1=((3, 4, 64, FS), BF16),
    ra1=((3, 4, 40, 512), BF16),
    rb1=((3, 4, 40, 384), BF16),
    sg1=((4, 64, FS), BF16),
    su1=((4, 64, FS), BF16),
    sa1=((4, 40, 512), BF16),
    sb1=((4, 40, 384), BF16),
    rg2=((3, 64, FS), BF16),
    ru2=((3, 64, FS), BF16),
    ra2=((3, 40, 512), BF16),
    rb2=((3, 40, 384), BF16),
    fs=((8, 2, 8, FS), F32),
    fr=((8, 2, 8, FS), F32),
    dkv=((2, T, 256), BF16),
    dkvf=((2, T, 256), F32),
    dkr=((T, 256), BF16),
    gat=((8, 4, 4, 4, 16, 256), BF16),
    gar=((4, 4, 4, 4, 16, 256), BF16),
    r1=((4, 3, 4, 4, 16, 256), BF16),
    t2=((4, 4, 4, 16, 256), BF16),
    r2=((4, 3, 4, 16, 256), BF16),
    t3=((4, 4, 16, 256), BF16),
    r3=((4, 3, 16, 256), BF16),
    fin=((4, 16, 256), F32),
    finr=((4, 8, 256), F32),
)
NSEM = 200


def body(tok, seg, gain_attn, wq, wk, wv, bias_qkv, wo, gain_ffn, wgate, wup, wdown, cot,
         out, ing, g_gain_attn, g_wq, g_wk, g_wv, g_bias, g_wo, g_gain_ffn, g_gate, g_up, g_down, *rest):
    s = dict(zip(SCRATCH, rest))
    ssem, rsem = rest[len(SCRATCH):]
    count = [0]
    sends = []
    di, yh = lax.axis_index("dp"), lax.axis_index("ctx")
    c, z, yl, x = di % 2, (di // 2) % 4, (di // 8) % 2, di // 16
    y = yh * 2 + yl
    here = {"x": x, "y": y, "z": z}

    def device(x, y, z, c):
        return (((x * 2 + y % 2) * 4 + z) * 2 + c, y // 2)

    def along(axis, k):
        at = dict(here)
        at[axis] = (at[axis] + k) % 4
        return device(at["x"], at["y"], at["z"], c)

    sibling = device(x, y, z, 1 - c)

    def remote(src, dst, dev):
        n = count[0]
        count[0] += 1
        copy = pltpu.make_async_remote_copy(
            src_ref=src, dst_ref=dst, send_sem=ssem.at[n], recv_sem=rsem.at[n],
            device_id=dev, device_id_type=MESH)
        copy.start()
        sends.append(copy)
        return copy

    def landed(copies):
        for copy in copies:
            copy.wait_recv()

    barrier = pltpu.get_barrier_semaphore()
    partners = [along(axis, k) for axis in "xyz" for k in (1, 2, 3)] + [sibling]
    partners += [device(x, (y + k) % 4, z, 1 - c) for k in (1, 2, 3)]
    for dev in partners:
        pl.semaphore_signal(barrier, inc=1, device_id=dev, device_id_type=MESH)

    pkf = s["pkf"]
    pkf[0:7, 0:896] = wq[...].astype(F32)
    pkf[0:7, 896:1024] = wk[...].astype(F32)
    pkf[0:7, 1024:1152] = wv[...].astype(F32)
    pkf[0:7, 1152:2048] = wo[...].astype(F32)
    pkf[7:8, :] = jnp.zeros((1, 2048), F32)
    pkf[7:8, 0:7] = gain_attn[...].astype(F32)
    pkf[7:8, 7:14] = gain_ffn[...].astype(F32)
    pkf[7:8, 14:23] = bias_qkv[...].astype(F32)
    for p in range(4):
        s["pk"][p] = jnp.concatenate(
            [pkf[:, 256 * p:256 * p + 256], pkf[:, 1024 + 256 * p:1280 + 256 * p]], axis=0).astype(BF16)
    s["segs"][yh] = jnp.broadcast_to(seg[...], (8, 128))
    s["yall"][y, c] = cot[...]

    pad, order, pick, mask = s["pad"], s["order"], s["pick"], s["mask"]
    r = iota((FS, 1), 0)
    u = lax.shift_right_logical(r * 1725, 16)
    target = (u & 3) * 160 + (u >> 2) * 40 + (r - u * 38)
    order[...] = one_hot((iota((FS, FS), 1) == target) & (r < 608))

    pl.semaphore_wait(barrier, len(partners))
    swap = remote(s["pk"], s["pkr"], sibling)
    seg_copy = remote(s["segs"].at[yh], s["segs"].at[yh], along("y", 2))

    guf = s["guf"]
    guf[...] = jnp.zeros(guf.shape, F32)
    for k in range(8):
        guf[0, k, 0:7, 0:608] = wgate[:, 608 * k:608 * k + 608].astype(F32)
        guf[1, k, 0:7, 0:608] = wup[:, 608 * k:608 * k + 608].astype(F32)
    placed = mm(guf[...].reshape(128, FS).astype(BF16), order[...]).reshape(2, 4, 2, 8, FS)
    lane = iota((32, FS), 1)
    for q in range(4):
        piece = jnp.zeros((32, FS), F32)
        for xx in range(4):
            moved = placed[:, xx].reshape(32, FS)
            if xx != q:
                moved = pltpu.roll(moved, (160 * (xx - q)) % FS, 1)
            piece = jnp.where((lane >= 160 * xx) & (lane < 160 * xx + 160), moved, piece)
        piece = piece.reshape(2, 2, 8, FS)
        for yy in range(2):
            s["gus"][(2 * (q % 2) + yy) * 2 + q // 2] = jnp.concatenate(
                [piece[0, yy], piece[1, yy]], axis=0).astype(BF16)
    me8 = y * 2 + c
    gu_in = []
    for k in range(4):
        for e in range(2):
            if k or e:
                ty, tc = (y + k) % 4, (c + e) % 2
                gu_in.append(remote(s["gus"].at[ty * 2 + tc], s["gui"].at[me8], device(x, ty, z, tc)))
    s["gui"][me8] = s["gus"][me8]

    swap.wait_recv()
    for p in range(4):
        own, other = s["pk"][p].astype(F32), s["pkr"][p].astype(F32)
        first = jnp.concatenate([own[0:8], other[0:8]], axis=0)
        second = jnp.concatenate([other[8:16], own[8:16]], axis=0)
        s["aw"][4 * c + p, x, z, y] = jnp.where(c == 0, first, second).astype(BF16)

    def region(ref, axes):
        at = [here[a] if a not in axes else slice(None) for a in "xzy"]
        return ref.at[tuple(at)]

    def attn_phase(phase):
        copies = []
        for p, axes in enumerate(ORDERS):
            part = region(s["aw"].at[4 * c + p], axes[:phase])
            copies.append([remote(part, part, along(axes[phase], k)) for k in (1, 2, 3)])
        return copies

    first = attn_phase(0)

    wdf = s["wdf"]
    wdf[0:38] = wdown[...].astype(F32)
    wdf[38:40] = jnp.zeros((2, D), F32)
    s["da"][x, z] = wdf[:, 0:512].astype(BF16)
    s["db"][x, z] = wdf[:, 512:896].astype(BF16)
    landed(gu_in)
    for yy in range(4):
        even, odd = s["gui"][2 * yy].astype(F32), s["gui"][2 * yy + 1].astype(F32)
        rows = pl.ds(16 * yy, 16)
        s["wg"][x, z, rows] = jnp.concatenate([even[0:8], odd[0:8]], axis=0).astype(BF16)
        s["wu"][x, z, rows] = jnp.concatenate([even[8:16], odd[8:16]], axis=0).astype(BF16)

    def ffn_phase(phase):
        copies = []
        for name, axes in (("wg", "xz"), ("wu", "zx"), ("da", "xz"), ("db", "zx")):
            at = [here[a] if a not in axes[:phase] else slice(None) for a in "xz"]
            part = s[name].at[tuple(at)]
            copies += [remote(part, part, along(axes[phase], k)) for k in (1, 2, 3)]
        return copies

    ffn1 = ffn_phase(0)
    for at in range(0, D, 128):
        d = iota((128, 1), 0) + at
        i = sevenths(d)
        pad[at:at + 128] = one_hot(iota((128, DP), 1) == slot_of(i) * 8 + (d - i * 7))
    for group in first:
        landed(group)
    second = attn_phase(1)
    landed(ffn1)
    ffn2 = ffn_phase(1)
    for group in second:
        landed(group)
    third = attn_phase(2)

    ymine = s["yall"].at[y, c]
    y_sib = remote(ymine, ymine, sibling)
    y_ring = [remote(ymine, ymine, along("y", k)) for k in (1, 2, 3)]

    xf = tok[...].astype(F32)
    r1 = lax.rsqrt(jnp.mean(xf * xf, axis=-1, keepdims=True) + EPS)
    seg_copy.wait_recv()
    rows0 = s["segs"][0][0:1].astype(F32)
    rows1 = s["segs"][1][0:1].astype(F32)
    own_row = jnp.where(yh == 0, rows0, rows1)
    diag = iota((T, T), 0) == iota((T, T), 1)
    own_seg = jnp.sum(jnp.where(diag, own_row, 0.0), axis=1, keepdims=True)
    length = jnp.sum(2.0 * T - jnp.sum(rows0 + rows1, axis=1, keepdims=True), axis=0, keepdims=True)
    base = (yh * T).astype(F32)
    place = iota((T, 128), 0).astype(F32) + base
    lane128 = iota((T, 128), 1)
    expo = (lane128 % 32).astype(F32) * (-2.0 / 64.0)
    freq = jnp.exp(expo * float(np.log(1e6)))
    angle = (place - own_seg * length) * freq
    cosine = jnp.cos(angle)
    low_half = lane128 % 64 < 32
    sine = jnp.where(low_half, -jnp.sin(angle), jnp.sin(angle))

    def swapped(v):
        return jnp.where(low_half, pltpu.roll(v, 96, 1), pltpu.roll(v, 32, 1))

    key_seg = jnp.concatenate([rows0, rows1], axis=1)
    key_at = iota((T, 256), 1)
    query_at = iota((T, 256), 0) + yh * T
    allowed = (key_seg == own_seg) & (key_at <= query_at)
    last_rows = one_hot(iota((128, DP), 1) == iota((128, DP), 0) * 8 + 7)
    n = iota((1, VEC), 1)
    d = jnp.where(n >= D, n - D, n)
    i = sevenths(d)
    m = n - 2 * D
    im = ninths(m)
    lane_of = jnp.where(m >= 0, 14 + m - im * 9, d - i * 7 + jnp.where(n >= D, 7, 0))
    pick[...] = one_hot(iota((32, VEC), 0) == lane_of)
    mask[...] = one_hot(iota((128, VEC), 0) == slot_of(jnp.where(m >= 0, im, i)))

    forward = []
    for p, axes in enumerate(ORDERS):
        part = region(s["aw"].at[4 * c + p], axes[:2])
        forward.append(remote(part, part, sibling))
    for k in (1, 2, 3):
        for p, axes in enumerate(ORDERS):
            third[p][k - 1].wait_recv()
            at = [slice(None)] * 3
            at["xzy".index(axes[2])] = (here[axes[2]] - k) % 4
            part = s["aw"].at[4 * c + p].at[tuple(at)]
            forward.append(remote(part, part, sibling))
    landed(forward)

    def weight(g):
        return s["aw"][g].reshape(DP, 256)

    picked = mm(last_rows, weight(0)[:, 0:128])[:, 0:32].astype(BF16)
    vecs = jnp.sum(mm(picked, pick[...]) * mask[...].astype(F32), axis=0, keepdims=True)
    gain_a, gain_f, bias = vecs[:, 0:D], vecs[:, D:2 * D], vecs[:, 2 * D:]

    a = (xf * r1 * gain_a).astype(BF16)
    a_pad = mm(a, pad[...]).astype(BF16)
    qkv = [mm(a_pad, weight(g)) for g in range(4)]
    qkv.append(mm(a_pad, weight(4)[:, 0:128]))

    def tile(t):
        v = qkv[t // 2] if t == 8 else qkv[t // 2][:, 128 * (t % 2):128 * (t % 2) + 128]
        return v + bias[:, 128 * t:128 * t + 128]

    def rope(v):
        return v * cosine + swapped(v) * sine

    key_tile = rope(tile(7)).astype(BF16)
    value_tile = tile(8).astype(BF16)
    s["kv"][yh] = jnp.concatenate([key_tile, value_tile], axis=1)
    kv_copy = remote(s["kv"].at[yh], s["kv"].at[yh], along("y", 2))
    q_tiles = [rope(tile(t)).astype(BF16) for t in range(7)]

    y_fwd = []
    for k in (1, 2, 3):
        y_ring[k - 1].wait_recv()
        part = s["yall"].at[(y - k) % 4, c]
        y_fwd.append(remote(part, part, sibling))

    kv_copy.wait_recv()
    kv = s["kv"][...].reshape(256, 256).astype(F32)
    lane256 = iota((256, 128), 1)

    def halves(v):
        turned = pltpu.roll(v, 64, 1)
        lo, hi = lane256 < 64, lane256 >= 64
        pick2 = lambda m, u: jnp.where(m, u, 0.0).astype(BF16)
        return ((pick2(lo, v), pick2(hi, turned)), (pick2(lo, turned), pick2(hi, v)))

    keys = halves(kv[:, 0:128])
    values = halves(kv[:, 128:256])
    mixed = []
    for t in range(7):
        total = None
        for e in range(2):
            h = 2 * t + e
            logits = jnp.where(allowed, mm_nt(q_tiles[t], keys[h // 7][e]) * 0.125, MASKED)
            top = jnp.max(logits, axis=-1, keepdims=True)
            raw = jnp.exp(logits - top)
            pr = raw / jnp.sum(raw, axis=-1, keepdims=True)
            s["prob"][h] = pr
            part = mm(pr.astype(BF16), values[h // 7][e])
            total = part if total is None else total + part
        mixed.append(total.astype(BF16))
    mixed = jnp.concatenate(mixed, axis=1)
    o_pad = mm(mixed, pad[...]).astype(BF16)
    att = jnp.concatenate(
        [mm(o_pad, weight(4)[:, 128:256])] + [mm(o_pad, weight(g)) for g in (5, 6, 7)], axis=1)
    hidden = xf + att
    r2 = lax.rsqrt(jnp.mean(hidden * hidden, axis=-1, keepdims=True) + EPS)
    b = (hidden * r2 * gain_f).astype(BF16)
    s["ball"][y, c] = mm(b, pad[...]).astype(BF16)
    bmine = s["ball"].at[y, c]
    b_sib = remote(bmine, bmine, sibling)
    b_ring = [remote(bmine, bmine, along("y", k)) for k in (1, 2, 3)]

    landed(ffn2)
    b_fwd = []
    for k in (1, 2, 3):
        b_ring[k - 1].wait_recv()
        part = s["ball"].at[(y - k) % 4, c]
        b_fwd.append(remote(part, part, sibling))
    landed([y_sib, b_sib] + y_fwd)

    base = count[0]
    count[0] += 16

    def chunk_copies(k):
        yy = (y + k) % 4
        copies = []
        for j, (part, got, ring) in enumerate((("pd", "qd", "rd"), ("po", "qo", "ro"))):
            n = base + 8 * j + k
            copies.append(pltpu.make_async_remote_copy(
                src_ref=s[part].at[yy, 1 - c], dst_ref=s[got].at[yy], send_sem=ssem.at[n], recv_sem=rsem.at[n],
                device_id=sibling, device_id_type=MESH))
            copies.append(pltpu.make_async_remote_copy(
                src_ref=s[part].at[yy, c], dst_ref=s[ring].at[k - 1], send_sem=ssem.at[n + 4],
                recv_sem=rsem.at[n + 4], device_id=along("y", k), device_id_type=MESH))
        return copies

    def chunk(step, carry):
        k = 3 - step
        d_sib, d_ring, o_sib, o_ring = chunk_copies(k)
        yy = (y + k) % 4
        bt = s["ball"][yy].reshape(2 * T, DP)
        yt = s["yall"][yy].reshape(2 * T, D)
        gate_w, up_w = s["wg"][...].reshape(DP, FS), s["wu"][...].reshape(DP, FS)
        down_a, down_b = s["da"][...].reshape(FS, 512), s["db"][...].reshape(FS, 384)
        gate, up = mm(bt, gate_w), mm(bt, up_w)
        sg = 1.0 / (1.0 + jnp.exp(-gate))
        silu = gate * sg
        m = (silu * up).astype(BF16)
        dm = mm_nt(yt[:, 0:512], down_a) + mm_nt(yt[:, 512:896], down_b)
        dgate = (dm * up * sg * (1.0 + gate * (1.0 - sg))).astype(BF16)
        dup = (dm * silu).astype(BF16)
        s["mb"][yy], s["dgb"][yy], s["dub"][yy] = m, dgate, dup
        s["pd"][yy] = (mm_nt(dgate, gate_w) + mm_nt(dup, up_w)).astype(BF16).reshape(2, T, DP)
        d_sib.start()
        s["po"][yy, :, :, 0:512] = mm(m, down_a).astype(BF16).reshape(2, T, 512)
        s["po"][yy, :, :, 512:896] = mm(m, down_b).astype(BF16).reshape(2, T, 384)
        o_sib.start()
        d_sib.wait_recv()
        s["pd"][yy, c] = (s["pd"][yy, c].astype(F32) + s["qd"][yy].astype(F32)).astype(BF16)

        @pl.when(k > 0)
        def _():
            d_ring.start()

        o_sib.wait_recv()
        s["po"][yy, c] = (s["po"][yy, c].astype(F32) + s["qo"][yy].astype(F32)).astype(BF16)

        @pl.when(k > 0)
        def _():
            o_ring.start()

        return carry

    landed(b_fwd)
    lax.fori_loop(0, 4, chunk, 0)
    red_d, red_o = [], []
    for k in range(4):
        d_sib, d_ring, o_sib, o_ring = chunk_copies(k)
        sends.extend([d_sib, o_sib])
        if k:
            sends.extend([d_ring, o_ring])
            red_d.append(d_ring)
            red_o.append(o_ring)

    ball = s["ball"][...].reshape(1024, DP)
    s["gg"][...] = mm_tn(ball, s["dgb"][...].reshape(1024, FS)).astype(BF16).reshape(4, 4, 64, FS)
    s["gu"][...] = mm_tn(ball, s["dub"][...].reshape(1024, FS)).astype(BF16).reshape(4, 4, 64, FS)
    down = mm_tn(s["mb"][...].reshape(1024, FS), s["yall"][...].reshape(1024, D))
    s["ga"][...] = down[:, 0:512].reshape(4, 4, 40, 512).astype(BF16)
    s["gb"][...] = down[:, 512:896].reshape(4, 4, 40, 384).astype(BF16)
    FG = (("gg", "rg1", "sg1", "rg2", "zx"), ("gu", "ru1", "su1", "ru2", "xz"),
          ("ga", "ra1", "sa1", "ra2", "zx"), ("gb", "rb1", "sb1", "rb2", "xz"))

    def plane(ref, axis, index):
        return ref.at[index] if axis == "x" else ref.at[:, index]

    fg1 = []
    for src, r_1, s_1, r_2, axes in FG:
        for k in (1, 2, 3):
            there = (here[axes[0]] + k) % 4
            fg1.append(remote(plane(s[src], axes[0], there), s[r_1].at[k - 1], along(axes[0], k)))

    landed(red_d)
    db_pad = s["pd"][y, c].astype(F32)
    for k in (1, 2, 3):
        db_pad = db_pad + s["rd"][k - 1].astype(F32)
    hi, lo = split(db_pad)
    dbv = mm_nt(hi, pad[...]) + mm_nt(lo, pad[...])
    gain_f_grad = jnp.sum(dbv * hidden * r2, axis=0, keepdims=True)
    ev = dbv * gain_f
    inner = jnp.mean(ev * hidden, axis=-1, keepdims=True)
    dh = cot[...].astype(F32) + r2 * ev - hidden * (r2 * r2 * r2 * inner)
    dh_low = dh.astype(BF16)
    do_pad = mm_nt(dh_low[:, 0:128], weight(4)[:, 128:256])
    for g in (5, 6, 7):
        at = 128 + 256 * (g - 5)
        do_pad = do_pad + mm_nt(dh_low[:, at:at + 256], weight(g))
    do = mm_nt(do_pad.astype(BF16), pad[...]).astype(BF16)

    dk = [[None, None], [None, None]]
    dv = [[None, None], [None, None]]
    dq_tiles = []
    for t in range(7):
        do_t = do[:, 128 * t:128 * t + 128]
        total = None
        for e in range(2):
            h = 2 * t + e
            g = h // 7
            pr = s["prob"][h]
            dpr = mm_nt(do_t, values[g][e])
            ds = (pr * (dpr - jnp.sum(pr * dpr, axis=-1, keepdims=True)) * 0.125).astype(BF16)
            part = mm(ds, keys[g][e])
            total = part if total is None else total + part
            kp, vp = mm_tn(ds, q_tiles[t]), mm_tn(pr.astype(BF16), do_t)
            dk[g][e] = kp if dk[g][e] is None else dk[g][e] + kp
            dv[g][e] = vp if dv[g][e] is None else dv[g][e] + vp
        dq_tiles.append((total * cosine - swapped(total) * sine).astype(BF16))

    def gather(parts):
        lo = parts[0][0] + pltpu.roll(parts[0][1], 64, 1)
        hi = parts[1][1] + pltpu.roll(parts[1][0], 64, 1)
        return jnp.where(lane256 < 64, lo, hi)

    dkv = jnp.concatenate([gather(dk), gather(dv)], axis=1).reshape(2, T, 256)
    s["dkvf"][...] = dkv
    s["dkv"][...] = dkv.astype(BF16)
    dkv_copy = remote(s["dkv"].at[1 - yh], s["dkr"], along("y", 2))

    landed(red_o)
    total = hidden + s["po"][y, c].astype(F32)
    for k in (1, 2, 3):
        total = total + s["ro"][k - 1].astype(F32)
    out[...] = total.astype(BF16)

    def grad(g, value):
        s["gat"][g] = value.astype(BF16).reshape(4, 4, 4, 16, 256)

    out_grad = mm_tn(o_pad, dh_low)
    for g in (5, 6, 7):
        at = 128 + 256 * (g - 5)
        grad(g, out_grad[:, at:at + 256])
    dq = jnp.concatenate(dq_tiles, axis=1)
    dkv_copy.wait_recv()
    dkv_own = s["dkvf"][yh] + s["dkr"][...].astype(F32)
    dko, dvl = dkv_own[:, 0:128], dkv_own[:, 128:256].astype(BF16)
    dkl = (dko * cosine - swapped(dko) * sine).astype(BF16)
    dqkv = jnp.concatenate([dq, dkl, dvl], axis=1)
    da_pad = mm_nt(dqkv[:, 1024:1152], weight(4)[:, 0:128])
    for g in range(4):
        da_pad = da_pad + mm_nt(dqkv[:, 256 * g:256 * g + 256], weight(g))
    hi, lo = split(da_pad)
    dav = mm_nt(hi, pad[...]) + mm_nt(lo, pad[...])
    gain_a_grad = jnp.sum(dav * xf * r1, axis=0, keepdims=True)
    bias_grad = jnp.sum(dqkv.astype(F32), axis=0, keepdims=True)
    small = jnp.concatenate([gain_a_grad, gain_f_grad, bias_grad], axis=1)
    spread = (mask[...].astype(F32) * small).astype(BF16)
    small_rows = mm_nt(spread, pick[...]).astype(BF16)
    small_rows = mm_tn(last_rows, jnp.concatenate([small_rows, jnp.zeros((128, 96), BF16)], axis=1))
    for g in range(4):
        value = mm_tn(a_pad, dqkv[:, 256 * g:256 * g + 256])
        if g == 0:
            value = jnp.concatenate([value[:, 0:128] + small_rows, value[:, 128:256]], axis=1)
        grad(g, value)
    grad(4, jnp.concatenate([mm_tn(a_pad, dvl), out_grad[:, 0:128]], axis=1))
    gat_copy = remote(s["gat"].at[pl.ds((1 - c) * 4, 4)], s["gar"], sibling)

    fv = dav * gain_a
    inner = jnp.mean(fv * xf, axis=-1, keepdims=True)
    ing[...] = (dh + r1 * fv - xf * (r1 * r1 * r1 * inner)).astype(BF16)

    gat_copy.wait_recv()
    for p in range(4):
        s["gat"][4 * c + p] = (s["gat"][4 * c + p].astype(F32) + s["gar"][p].astype(F32)).astype(BF16)

    def cut(axes, axis, index):
        order3 = [a for a in "xzy" if a in axes]
        at = [slice(None)] * len(order3)
        at[order3.index(axis)] = index
        return tuple(at)

    def reduce_phase(src, dst, phase):
        copies = []
        for p, axes in enumerate(ORDERS):
            left, axis = axes[:3 - phase], axes[2 - phase]
            for k in (1, 2, 3):
                there = (here[axis] + k) % 4
                part = s[src].at[4 * c + p if src == "gat" else p].at[cut(left, axis, there)]
                copies.append(remote(part, s[dst].at[p, k - 1], along(axis, k)))
        return copies

    def reduce_sum(src, dst, phase):
        sums = []
        for p, axes in enumerate(ORDERS):
            left, axis = axes[:3 - phase], axes[2 - phase]
            total = s[src][(4 * c + p if src == "gat" else p,) + cut(left, axis, here[axis])].astype(F32)
            for k in (1, 2, 3):
                total = total + s[dst][p, k - 1].astype(F32)
            sums.append(total)
        return sums

    ph1 = reduce_phase("gat", "r1", 0)

    landed(fg1)
    fg2 = []
    for src, r_1, s_1, r_2, axes in FG:
        own = s[src][here["x"]] if axes[0] == "x" else s[src][:, here["z"]]
        total = own.astype(F32)
        for k in (1, 2, 3):
            total = total + s[r_1][k - 1].astype(F32)
        s[s_1][...] = total.astype(BF16)
        for k in (1, 2, 3):
            there = (here[axes[1]] + k) % 4
            fg2.append(remote(s[s_1].at[there], s[r_2].at[k - 1], along(axes[1], k)))

    landed(ph1)
    for p, total in enumerate(reduce_sum("gat", "r1", 0)):
        s["t2"][p] = total.astype(BF16)
    ph2 = reduce_phase("t2", "r2", 1)

    landed(fg2)
    sums = []
    for src, r_1, s_1, r_2, axes in FG:
        total = s[s_1][here[axes[1]]].astype(F32)
        for k in (1, 2, 3):
            total = total + s[r_2][k - 1].astype(F32)
        sums.append(total)
    g_down[:, 0:512] = sums[2][0:38]
    g_down[:, 512:896] = sums[3][0:38]
    s["fs"][:, 0] = sums[0].reshape(8, 8, FS)
    s["fs"][:, 1] = sums[1].reshape(8, 8, FS)
    fin_in = []
    for k in range(4):
        for e in range(2):
            if k or e:
                ty, tc = (y + k) % 4, (c + e) % 2
                fin_in.append(remote(s["fs"].at[ty * 2 + tc], s["fr"].at[me8], device(x, ty, z, tc)))
    s["fr"][me8] = s["fs"][me8]

    landed(ph2)
    for p, total in enumerate(reduce_sum("t2", "r2", 1)):
        s["t3"][p] = total.astype(BF16)
    ph3 = reduce_phase("t3", "r3", 2)

    landed(fin_in)
    for yy in range(2):
        for xx in range(4):
            block = jnp.zeros((16, FS), F32)
            lane16 = iota((16, FS), 1)
            for q in range(4):
                moved = s["fr"][(2 * (q % 2) + yy) * 2 + q // 2].reshape(16, FS)
                if xx != q:
                    moved = pltpu.roll(moved, (160 * (q - xx)) % FS, 1)
                block = jnp.where((lane16 >= 160 * q) & (lane16 < 160 * q + 160), moved, block)
            guf[:, 2 * xx + yy] = block.reshape(2, 8, FS)
    hi, lo = split(guf[...].reshape(128, FS))
    flat = (mm_nt(hi, order[...]) + mm_nt(lo, order[...])).reshape(2, 8, 8, FS)
    for g, ref in enumerate((g_gate, g_up)):
        for k in range(8):
            ref[:, 608 * k:608 * k + 608] = flat[g, k, 0:7, 0:608]

    landed(ph3)
    for p, total in enumerate(reduce_sum("t3", "r3", 2)):
        s["fin"][p] = total
    fin_copy = remote(s["fin"].at[:, pl.ds((1 - c) * 8, 8)], s["finr"], sibling)
    fin_copy.wait_recv()
    for p in range(4):
        own = jnp.where(c == 0, s["fin"][p, 0:8], s["fin"][p, 8:16])
        other = s["finr"][p]
        pkf[:, 256 * p:256 * p + 256] = jnp.where(c == 0, own, other)
        pkf[:, 1024 + 256 * p:1280 + 256 * p] = jnp.where(c == 0, other, own)
    g_wq[...] = pkf[0:7, 0:896]
    g_wk[...] = pkf[0:7, 896:1024]
    g_wv[...] = pkf[0:7, 1024:1152]
    g_wo[...] = pkf[0:7, 1152:2048]
    g_gain_attn[...] = pkf[7:8, 0:7]
    g_gain_ffn[...] = pkf[7:8, 7:14]
    g_bias[...] = pkf[7:8, 14:23]
    for copy in sends:
        copy.wait_send()
    assert count[0] <= NSEM, count[0]


def per_device(*args):
    vmem = pl.BlockSpec(memory_space=pltpu.VMEM)
    shapes = [((T, D), BF16), ((T, D), BF16), ((1, 7), F32), ((7, D), F32), ((7, 128), F32), ((7, 128), F32),
              ((1, 9), F32), ((7, D), F32), ((1, 7), F32), ((7, FF), F32), ((7, FF), F32), ((38, D), F32)]
    results = pl.pallas_call(
        body,
        out_shape=tuple(jax.ShapeDtypeStruct(shape, dtype) for shape, dtype in shapes),
        in_specs=[vmem] * 13,
        out_specs=(vmem,) * 12,
        scratch_shapes=[pltpu.VMEM(shape, dtype) for shape, dtype in SCRATCH.values()]
        + [pltpu.SemaphoreType.DMA((NSEM,)), pltpu.SemaphoreType.DMA((NSEM,))],
        compiler_params=pltpu.CompilerParams(
            collective_id=0, has_side_effects=True, vmem_limit_bytes=60 * 2**20),
        name="layer",
    )(*(v.reshape(1, -1) if v.ndim == 1 else v for v in args))
    return tuple(v.reshape(-1) if v.shape[0] == 1 else v for v in results)


def solution(mesh):
    both = P(("dp", "ctx"))
    rows = P(("dp", "ctx"), None)
    return jax.shard_map(
        per_device,
        mesh=mesh,
        in_specs=(rows, both, both, rows, rows, rows, both, rows, both, rows, rows, rows, rows),
        out_specs=(rows, rows, both, rows, rows, rows, both, rows, both, rows, rows, rows),
        check_vma=False,
    )
```

```python
import functools

import jax
import jax.numpy as jnp
import numpy as np
from jax import lax
from jax.experimental import pallas as pl
from jax.experimental.pallas import tpu as pltpu
from jax.sharding import PartitionSpec as P

F32 = jnp.float32
BF16 = jnp.bfloat16
MESH = pl.DeviceIdType.MESH
D = 896
DP = 1024
FF = 4864
FS = 640
T = 128
VEC = 2 * D + 1152
EPS = 1e-6
MASKED = -1e9
LANES = (0, 128, 256, 384, 896, 1280, 1408, 1536, 512, 640, 768, 1024, 1152, 1664, 1792, 1920)
QUERY, KEY, VALUE, OUT = (0, 1, 2, 3, 8, 9, 10), 4, 11, (12, 5, 6, 7, 13, 14, 15)
GATHER1 = ((0, 2, "xzy"), (2, 1, "zxy"), (3, 1, "yxz"), (4, 1, "yzx"))
GATHER2 = ((5, 1, "xzy"), (6, 1, "zxy"), (7, 1, "yxz"))
REDUCE = (((5, 2, "xzy"), (7, 1, "zxy")), ((0, 2, "xzy"), (2, 1, "zxy")), ((3, 1, "yxz"), (4, 1, "yzx")))


def iota(shape, axis):
    return lax.broadcasted_iota(jnp.int32, shape, axis)


def sevenths(v):
    return lax.shift_right_logical(v * 9363, 16)


def ninths(v):
    return lax.shift_right_logical(v * 7282, 16)


def slot_of(i):
    return (i >> 5) * 32 + ((i >> 2) & 3) * 8 + (i & 1) * 4 + ((i >> 4) & 1) * 2 + ((i >> 1) & 1)


def one_hot(test):
    return jnp.where(test, 1.0, 0.0).astype(BF16)


def mm(a, b):
    return jnp.dot(a, b, preferred_element_type=F32)


def mm_nt(a, b):
    return lax.dot_general(a, b, (((1,), (1,)), ((), ())), preferred_element_type=F32)


def mm_tn(a, b):
    return lax.dot_general(a, b, (((0,), (0,)), ((), ())), preferred_element_type=F32)


def split(v):
    hi = v.astype(BF16)
    return hi, (v - hi.astype(F32)).astype(BF16)


INPUTS = dict(
    tok=((T, D), BF16), seg=((1, T), jnp.int32), gain_attn=((1, 7), BF16), wq=((7, D), BF16), wk=((7, 128), BF16),
    wv=((7, 128), BF16), bias_qkv=((1, 9), BF16), wo=((7, D), BF16), gain_ffn=((1, 7), BF16), wgate=((7, FF), BF16),
    wup=((7, FF), BF16), wdown=((38, D), BF16), cot=((T, D), BF16),
)
OUTPUTS = dict(
    out=((T, D), BF16), ing=((T, D), BF16), g_gain_attn=((1, 7), F32), g_wq=((7, D), F32), g_wk=((7, 128), F32),
    g_wv=((7, 128), F32), g_bias=((1, 9), F32), g_wo=((7, D), F32), g_gain_ffn=((1, 7), F32), g_gate=((7, FF), F32),
    g_up=((7, FF), F32), g_down=((38, D), F32),
)
SCRATCH = dict(
    pkf=((8, 2048), F32),
    pk=((8, 16, 128), BF16),
    pkr=((8, 16, 128), BF16),
    aw=((16, 4, 4, 4, 16, 128), BF16),
    guf=((2, 8, 8, FS), F32),
    gus=((8, 16, FS), BF16),
    gui=((8, 16, FS), BF16),
    wf=((2, 56, FS), F32),
    wg=((4, 4, 56, FS), BF16),
    wu=((4, 4, 56, FS), BF16),
    da=((4, 4, 40, 512), BF16),
    db=((4, 4, 40, 384), BF16),
    pad=((D, DP), BF16),
    perm=((D, D), BF16),
    order=((FS, FS), BF16),
    pick=((32, VEC), BF16),
    mask=((128, VEC), BF16),
    wdf=((40, D), F32),
    segs=((2, 8, 128), jnp.int32),
    kv=((2, T, 256), BF16),
    prob=((14, T, 256), F32),
    ball=((4, 2, T, D), BF16),
    yall=((4, 2, T, D), BF16),
    mb=((4, 2 * T, FS), BF16),
    dgb=((4, 2 * T, FS), BF16),
    dub=((4, 2 * T, FS), BF16),
    po=((4, 2, T, D), BF16),
    pd=((4, 2, T, D), BF16),
    qo=((4, T, D), BF16),
    qd=((4, T, D), BF16),
    ro=((3, T, D), BF16),
    rd=((3, T, D), BF16),
    gg=((4, 4, 56, FS), BF16),
    gu=((4, 4, 56, FS), BF16),
    ga=((4, 4, 40, 512), BF16),
    gb=((4, 4, 40, 384), BF16),
    rg1=((3, 4, 56, FS), BF16),
    ru1=((3, 4, 56, FS), BF16),
    ra1=((3, 4, 40, 512), BF16),
    rb1=((3, 4, 40, 384), BF16),
    sg1=((4, 56, FS), BF16),
    su1=((4, 56, FS), BF16),
    sa1=((4, 40, 512), BF16),
    sb1=((4, 40, 384), BF16),
    rg2=((3, 56, FS), BF16),
    ru2=((3, 56, FS), BF16),
    ra2=((3, 40, 512), BF16),
    rb2=((3, 40, 384), BF16),
    fs=((8, 2, 8, FS), F32),
    fr=((8, 2, 8, FS), F32),
    dkv=((2, T, 256), BF16),
    dkvf=((2, T, 256), F32),
    dkr=((T, 256), BF16),
    gat=((16, 4, 4, 4, 16, 128), BF16),
    gar=((8, 4, 4, 4, 16, 128), BF16),
    r1=((3, 8, 4, 4, 16, 128), BF16),
    t2=((8, 4, 4, 16, 128), BF16),
    r2=((3, 8, 4, 16, 128), BF16),
    t3=((8, 4, 16, 128), BF16),
    r3=((3, 8, 16, 128), BF16),
    fin=((8, 16, 128), F32),
    finr=((8, 8, 128), F32),
)
NSEM = 270


def body(*refs):
    sizes = (len(INPUTS), len(OUTPUTS), len(SCRATCH), len(INPUTS), len(OUTPUTS), 4)
    parts = []
    for size in sizes:
        parts.append(refs[sum(map(len, parts)):][:size])
    s = dict(zip(SCRATCH, parts[2]))
    i_ = dict(zip(INPUTS, parts[3]))
    o_ = dict(zip(OUTPUTS, parts[4]))
    ssem, rsem, isem, osem = parts[5]
    loads = {
        name: pltpu.make_async_copy(ref, i_[name], isem.at[n]) for n, (name, ref) in enumerate(zip(INPUTS, parts[0]))}
    stores = {
        name: pltpu.make_async_copy(o_[name], ref, osem.at[n]) for n, (name, ref) in enumerate(zip(OUTPUTS, parts[1]))}

    def load(*names):
        for name in names:
            loads[name].wait()
        return [i_[name][...] for name in names]

    def store(name, value):
        o_[name][...] = value
        stores[name].start()

    count = [0]
    sends = []
    di, yh = lax.axis_index("dp"), lax.axis_index("ctx")
    c, z, yl, x = di % 2, (di // 2) % 4, (di // 8) % 2, di // 16
    y = yh * 2 + yl
    here = {"x": x, "y": y, "z": z}

    def device(x, y, z, c):
        return (((x * 2 + y % 2) * 4 + z) * 2 + c, y // 2)

    def along(axis, k):
        at = dict(here)
        at[axis] = (at[axis] + k) % 4
        return device(at["x"], at["y"], at["z"], c)

    sibling = device(x, y, z, 1 - c)

    def remote(src, dst, dev):
        n = count[0]
        count[0] += 1
        copy = pltpu.make_async_remote_copy(
            src_ref=src, dst_ref=dst, send_sem=ssem.at[n], recv_sem=rsem.at[n],
            device_id=dev, device_id_type=MESH)
        copy.start()
        sends.append(copy)
        return copy

    def landed(copies):
        for copy in copies:
            copy.wait_recv()

    barrier = pltpu.get_barrier_semaphore()
    partners = [along(axis, k) for axis in "xyz" for k in (1, 2, 3)] + [sibling]
    partners += [device(x, (y + k) % 4, z, 1 - c) for k in (1, 2, 3)]
    for dev in partners:
        pl.semaphore_signal(barrier, inc=1, device_id=dev, device_id_type=MESH)

    for name in ("wgate", "wup", "wq", "wk", "wv", "wo", "gain_attn", "gain_ffn", "bias_qkv", "wdown", "seg", "cot", "tok"):
        loads[name].start()

    pad, perm, order, pick, mask = s["pad"], s["perm"], s["order"], s["pick"], s["mask"]
    r = iota((FS, 1), 0)
    u = lax.shift_right_logical(r * 1725, 16)
    target = (u & 3) * 160 + (u >> 2) * 40 + (r - u * 38)
    order[...] = one_hot((iota((FS, FS), 1) == target) & (r < 608))
    guf = s["guf"]
    guf[...] = jnp.zeros(guf.shape, F32)

    load("wgate", "wup")
    for k in range(8):
        guf[0, k, 0:7, 0:608] = i_["wgate"][:, 608 * k:608 * k + 608].astype(F32)
        guf[1, k, 0:7, 0:608] = i_["wup"][:, 608 * k:608 * k + 608].astype(F32)
    placed = mm(guf[...].reshape(128, FS).astype(BF16), order[...]).reshape(2, 4, 2, 8, FS)
    lane = iota((32, FS), 1)
    for q in range(4):
        piece = jnp.zeros((32, FS), F32)
        for xx in range(4):
            moved = placed[:, xx].reshape(32, FS)
            if xx != q:
                moved = pltpu.roll(moved, (160 * (xx - q)) % FS, 1)
            piece = jnp.where((lane >= 160 * xx) & (lane < 160 * xx + 160), moved, piece)
        piece = piece.reshape(2, 2, 8, FS)
        for yy in range(2):
            s["gus"][(2 * (q % 2) + yy) * 2 + q // 2] = jnp.concatenate(
                [piece[0, yy], piece[1, yy]], axis=0).astype(BF16)
    me8 = y * 2 + c
    s["gui"][me8] = s["gus"][me8]
    pkf = s["pkf"]
    wq, wk, wv, wo, gain_attn, gain_ffn, bias_qkv = load(
        "wq", "wk", "wv", "wo", "gain_attn", "gain_ffn", "bias_qkv")
    pkf[0:7, 0:896] = wq.astype(F32)
    pkf[0:7, 896:1024] = wk.astype(F32)
    pkf[0:7, 1024:1152] = wv.astype(F32)
    pkf[0:7, 1152:2048] = wo.astype(F32)
    pkf[7:8, :] = jnp.zeros((1, 2048), F32)
    pkf[7:8, 896:903] = gain_attn.astype(F32)
    pkf[7:8, 903:910] = gain_ffn.astype(F32)
    pkf[7:8, 910:919] = bias_qkv.astype(F32)
    for t in range(8):
        s["pk"][t] = jnp.concatenate(
            [pkf[:, at:at + 128] for at in (LANES[t], LANES[8 + t])], axis=0).astype(BF16)
    wdf = s["wdf"]
    (wdown,) = load("wdown")
    wdf[0:38] = wdown.astype(F32)
    wdf[38:40] = jnp.zeros((2, D), F32)
    s["da"][x, z] = wdf[:, 0:512].astype(BF16)
    s["db"][x, z] = wdf[:, 512:896].astype(BF16)
    (seg,) = load("seg")
    s["segs"][yh] = jnp.broadcast_to(seg, (8, 128))

    pl.semaphore_wait(barrier, len(partners))
    swap = remote(s["pk"], s["pkr"], sibling)

    def slab(name, axes, **index):
        return s[name].at[tuple(index.get(a, here[a]) for a in "xz")]

    def ffn_first(names):
        copies = []
        for name, axes in names:
            part = slab(name, axes)
            copies += [remote(part, part, along(axes[0], k)) for k in (1, 3, 2)]
        return copies

    def ffn_near(names):
        copies = []
        for name, axes in names:
            part = slab(name, axes, **{axes[0]: slice(None)})
            copies += [remote(part, part, along(axes[1], k)) for k in (1, 3)]
        return copies

    def ffn_far(names, near):
        copies = []
        for at, (name, axes) in enumerate(names):
            for h, k in enumerate((1, 3)):
                near[2 * at + h].wait_recv()
                part = slab(name, axes, **{axes[0]: pl.ds(2 * h, 2), axes[1]: (here[axes[1]] - k) % 4})
                copies.append(remote(part, part, along(axes[1], k)))
        return copies

    DOWN, WIDE = (("da", "xz"), ("db", "zx")), (("wg", "xz"), ("wu", "zx"))
    gu_in = []
    for k in (2, 1, 3, 0):
        for e in range(2):
            if k or e:
                ty, tc = (y + k) % 4, (c + e) % 2
                gu_in.append(remote(s["gus"].at[ty * 2 + tc], s["gui"].at[me8], device(x, ty, z, tc)))
    down1 = ffn_first(DOWN)
    seg_copy = remote(s["segs"].at[yh], s["segs"].at[yh], along("y", 2))

    swap.wait_recv()
    for t in range(8):
        own, other = s["pk"][t].astype(F32), s["pkr"][t].astype(F32)
        first = jnp.concatenate([own[0:8], other[0:8]], axis=0)
        second = jnp.concatenate([other[8:16], own[8:16]], axis=0)
        s["aw"][8 * c + t, x, z, y] = jnp.where(c == 0, first, second).astype(BF16)

    def slots(name, start, runs, axes, **index):
        at = [index.get(a, slice(None) if a in axes else here[a]) for a in "xzy"]
        return s[name].at[(pl.ds(start, runs),) + tuple(at)]

    def attn_phase(group, phase):
        copies = []
        for start, runs, axes in group:
            part = slots("aw", 8 * c + start, runs, axes[:phase])
            copies += [remote(part, part, along(axes[phase], k)) for k in (1, 2, 3)]
        return copies

    first1 = attn_phase(GATHER1, 0)
    first2 = attn_phase(GATHER2, 0)

    landed(gu_in)
    for at in range(8):
        both = s["gui"][at].astype(F32)
        s["wf"][0, 7 * at:7 * at + 7] = both[0:7]
        s["wf"][1, 7 * at:7 * at + 7] = both[8:15]
    s["wg"][x, z] = s["wf"][0].astype(BF16)
    s["wu"][x, z] = s["wf"][1].astype(BF16)
    wide1 = ffn_first(WIDE)
    landed(first1)
    second1 = attn_phase(GATHER1, 1)
    landed(first2)
    second2 = attn_phase(GATHER2, 1)
    landed(down1)
    down2 = ffn_near(DOWN)
    for at in range(0, D, 128):
        d = iota((128, 1), 0) + at
        i = sevenths(d)
        pad[at:at + 128] = one_hot(iota((128, DP), 1) == slot_of(i) * 8 + (d - i * 7))
        perm[at:at + 128] = one_hot(iota((128, D), 1) == slot_of(i) * 7 + (d - i * 7))
    landed(second1)
    third1 = attn_phase(GATHER1, 2)
    landed(wide1)
    wide2 = ffn_near(WIDE)
    landed(second2)
    third2 = attn_phase(GATHER2, 2)

    (tok,) = load("tok")
    xf = tok.astype(F32)
    (cot,) = load("cot")
    s["yall"][y, c] = cot
    r1 = lax.rsqrt(jnp.mean(xf * xf, axis=-1, keepdims=True) + EPS)
    seg_copy.wait_recv()
    rows0 = s["segs"][0][0:1].astype(F32)
    rows1 = s["segs"][1][0:1].astype(F32)
    own_row = jnp.where(yh == 0, rows0, rows1)
    diag = iota((T, T), 0) == iota((T, T), 1)
    own_seg = jnp.sum(jnp.where(diag, own_row, 0.0), axis=1, keepdims=True)
    length = jnp.sum(2.0 * T - jnp.sum(rows0 + rows1, axis=1, keepdims=True), axis=0, keepdims=True)
    base = (yh * T).astype(F32)
    place = iota((T, 128), 0).astype(F32) + base
    lane128 = iota((T, 128), 1)
    expo = (lane128 % 32).astype(F32) * (-2.0 / 64.0)
    freq = jnp.exp(expo * float(np.log(1e6)))
    angle = (place - own_seg * length) * freq
    cosine = jnp.cos(angle)
    low_half = lane128 % 64 < 32
    sine = jnp.where(low_half, -jnp.sin(angle), jnp.sin(angle))

    def swapped(v):
        return jnp.where(low_half, pltpu.roll(v, 96, 1), pltpu.roll(v, 32, 1))

    key_seg = jnp.concatenate([rows0, rows1], axis=1)
    key_at = iota((T, 256), 1)
    query_at = iota((T, 256), 0) + yh * T
    allowed = (key_seg == own_seg) & (key_at <= query_at)
    last_rows = one_hot(iota((128, DP), 1) == iota((128, DP), 0) * 8 + 7)
    n = iota((1, VEC), 1)
    d = jnp.where(n >= D, n - D, n)
    i = sevenths(d)
    m = n - 2 * D
    im = ninths(m)
    lane_of = jnp.where(m >= 0, 14 + m - im * 9, d - i * 7 + jnp.where(n >= D, 7, 0))
    pick[...] = one_hot(iota((32, VEC), 0) == lane_of)
    mask[...] = one_hot(iota((128, VEC), 0) == slot_of(jnp.where(m >= 0, im, i)))

    def pass_on(group, arrivals):
        copies = []
        for start, runs, axes in group:
            part = slots("aw", 8 * c + start, runs, axes[:2])
            copies.append(remote(part, part, sibling))
        for k in (1, 2, 3):
            for at, (start, runs, axes) in enumerate(group):
                arrivals[3 * at + k - 1].wait_recv()
                part = slots("aw", 8 * c + start, runs, axes[:2], **{axes[2]: (here[axes[2]] - k) % 4})
                copies.append(remote(part, part, sibling))
        return copies

    landed(pass_on(GATHER1, third1))

    def weight(*tiles):
        return jnp.concatenate([s["aw"][g].reshape(DP, 128) for g in tiles], axis=1)

    picked = mm(last_rows, weight(KEY))[:, 0:32].astype(BF16)
    vecs = jnp.sum(mm(picked, pick[...]) * mask[...].astype(F32), axis=0, keepdims=True)
    gain_a, gain_f, bias = vecs[:, 0:D], vecs[:, D:2 * D], vecs[:, 2 * D:]

    a = (xf * r1 * gain_a).astype(BF16)
    a_pad = mm(a, pad[...]).astype(BF16)
    qkv = mm(a_pad, weight(*QUERY, KEY, VALUE)) + bias

    def tile(t):
        return qkv[:, 128 * t:128 * t + 128]

    def rope(v):
        return v * cosine + swapped(v) * sine

    key_tile = rope(tile(7)).astype(BF16)
    value_tile = tile(8).astype(BF16)
    s["kv"][yh] = jnp.concatenate([key_tile, value_tile], axis=1)
    kv_copy = remote(s["kv"].at[yh], s["kv"].at[yh], along("y", 2))
    q_tiles = [rope(tile(t)).astype(BF16) for t in range(7)]

    ring = count[0]
    passed = ring + 8
    count[0] += 16

    def arriving(name, k):
        n = ring + k + 4 * (name == "yall")
        mine = s[name].at[y, c]
        return pltpu.make_async_remote_copy(
            src_ref=mine, dst_ref=mine, send_sem=ssem.at[n], recv_sem=rsem.at[n],
            device_id=along("y", 4 - k), device_id_type=MESH)

    def passing(name, k):
        n = passed + k + 4 * (name == "yall")
        part = s[name].at[(y + k) % 4, c]
        return pltpu.make_async_remote_copy(
            src_ref=part, dst_ref=part, send_sem=ssem.at[n], recv_sem=rsem.at[n],
            device_id=sibling, device_id_type=MESH)

    passing("yall", 0).start()
    for k in (1, 3, 2):
        arriving("yall", k).start()
    forward2 = pass_on(GATHER2, third2)
    down3 = ffn_far(DOWN, down2)
    wide3 = ffn_far(WIDE, wide2)
    kv_copy.wait_recv()
    kv = s["kv"][...].reshape(256, 256).astype(F32)
    lane256 = iota((256, 128), 1)

    def halves(v):
        turned = pltpu.roll(v, 64, 1)
        lo, hi = lane256 < 64, lane256 >= 64
        pick2 = lambda m, u: jnp.where(m, u, 0.0).astype(BF16)
        return ((pick2(lo, v), pick2(hi, turned)), (pick2(lo, turned), pick2(hi, v)))

    keys = halves(kv[:, 0:128])
    values = halves(kv[:, 128:256])
    mixed = []
    for t in range(7):
        total = None
        for e in range(2):
            h = 2 * t + e
            logits = jnp.where(allowed, mm_nt(q_tiles[t], keys[h // 7][e]) * 0.125, MASKED)
            top = jnp.max(logits, axis=-1, keepdims=True)
            raw = jnp.exp(logits - top)
            pr = raw / jnp.sum(raw, axis=-1, keepdims=True)
            s["prob"][h] = pr
            part = mm(pr.astype(BF16), values[h // 7][e])
            total = part if total is None else total + part
        mixed.append(total.astype(BF16))
    mixed = jnp.concatenate(mixed, axis=1)
    o_pad = mm(mixed, pad[...]).astype(BF16)
    landed(forward2)
    hidden = xf + mm(o_pad, weight(*OUT))
    r2 = lax.rsqrt(jnp.mean(hidden * hidden, axis=-1, keepdims=True) + EPS)
    b = (hidden * r2 * gain_f).astype(BF16)
    s["ball"][y, c] = mm(b, perm[...]).astype(BF16)
    passing("ball", 0).start()
    for k in (1, 3, 2):
        arriving("ball", k).start()
    landed(down3 + wide3)
    base = count[0]
    count[0] += 16

    def chunk_copies(k):
        yy = (y + k) % 4
        copies = []
        for j, (part, got, ring) in enumerate((("pd", "qd", "rd"), ("po", "qo", "ro"))):
            n = base + 8 * j + k
            copies.append(pltpu.make_async_remote_copy(
                src_ref=s[part].at[yy, 1 - c], dst_ref=s[got].at[yy], send_sem=ssem.at[n], recv_sem=rsem.at[n],
                device_id=sibling, device_id_type=MESH))
            copies.append(pltpu.make_async_remote_copy(
                src_ref=s[part].at[yy, c], dst_ref=s[ring].at[k - 1], send_sem=ssem.at[n + 4],
                recv_sem=rsem.at[n + 4], device_id=along("y", k), device_id_type=MESH))
        return copies

    def turn(step):
        return step + (step // 2) * (5 - 2 * step)

    def chunk(step, carry):
        k = turn(step)
        passing("ball", k).wait_recv()
        passing("yall", k).wait_recv()
        d_sib, d_ring, o_sib, o_ring = chunk_copies(k)
        yy = (y + k) % 4
        bt = s["ball"][yy].reshape(2 * T, D)
        yt = s["yall"][yy].reshape(2 * T, D)
        gate_w, up_w = s["wg"][...].reshape(D, FS), s["wu"][...].reshape(D, FS)
        down_a, down_b = s["da"][...].reshape(FS, 512), s["db"][...].reshape(FS, 384)
        gate, up = mm(bt, gate_w), mm(bt, up_w)
        sg = 1.0 / (1.0 + jnp.exp(-gate))
        silu = gate * sg
        m = (silu * up).astype(BF16)
        dm = mm_nt(yt[:, 0:512], down_a) + mm_nt(yt[:, 512:896], down_b)
        dgate = (dm * up * sg * (1.0 + gate * (1.0 - sg))).astype(BF16)
        dup = (dm * silu).astype(BF16)
        s["mb"][yy], s["dgb"][yy], s["dub"][yy] = m, dgate, dup
        s["pd"][yy] = (mm_nt(dgate, gate_w) + mm_nt(dup, up_w)).astype(BF16).reshape(2, T, D)
        d_sib.start()
        s["po"][yy, :, :, 0:512] = mm(m, down_a).astype(BF16).reshape(2, T, 512)
        s["po"][yy, :, :, 512:896] = mm(m, down_b).astype(BF16).reshape(2, T, 384)
        o_sib.start()

        @pl.when(step < 3)
        def _():
            for name in ("yall", "ball"):
                arriving(name, turn(step + 1)).wait_recv()
                passing(name, turn(step + 1)).start()

        d_sib.wait_recv()
        s["pd"][yy, c] = (s["pd"][yy, c].astype(F32) + s["qd"][yy].astype(F32)).astype(BF16)

        @pl.when(step > 0)
        def _():
            d_ring.start()

        return carry

    lax.fori_loop(0, 4, chunk, 0)
    for name in ("ball", "yall"):
        sends.extend([passing(name, k) for k in range(4)] + [arriving(name, k) for k in (1, 2, 3)])
    red_d, red_o = [], []
    for k in range(4):
        d_sib, d_ring, o_sib, o_ring = chunk_copies(k)
        sends.extend([d_sib, o_sib])
        o_sib.wait_recv()
        yy = (y + k) % 4
        s["po"][yy, c] = (s["po"][yy, c].astype(F32) + s["qo"][yy].astype(F32)).astype(BF16)
        if k:
            o_ring.start()
            sends.extend([d_ring, o_ring])
            red_d.append(d_ring)
            red_o.append(o_ring)

    ball = s["ball"][...].reshape(1024, D)
    s["gg"][...] = mm_tn(ball, s["dgb"][...].reshape(1024, FS)).astype(BF16).reshape(4, 4, 56, FS)
    s["gu"][...] = mm_tn(ball, s["dub"][...].reshape(1024, FS)).astype(BF16).reshape(4, 4, 56, FS)
    down = mm_tn(s["mb"][...].reshape(1024, FS), s["yall"][...].reshape(1024, D))
    s["ga"][...] = down[:, 0:512].reshape(4, 4, 40, 512).astype(BF16)
    s["gb"][...] = down[:, 512:896].reshape(4, 4, 40, 384).astype(BF16)
    FG = (("gg", "rg1", "sg1", "rg2", "zx"), ("gu", "ru1", "su1", "ru2", "xz"),
          ("ga", "ra1", "sa1", "ra2", "zx"), ("gb", "rb1", "sb1", "rb2", "xz"))

    def plane(ref, axis, index):
        return ref.at[index] if axis == "x" else ref.at[:, index]


    def piece(name, axes, **index):
        return tuple(index.get(a, slice(None)) for a in "xz")

    half = []
    for src, r_1, s_1, r_2, axes in FG:
        for h, k in enumerate((1, 3)):
            part = s[src].at[piece(src, axes, **{axes[0]: (here[axes[0]] + 2) % 4, axes[1]: pl.ds(2 * h, 2)})]
            half.append(remote(part, s[r_1].at[2, pl.ds(2 * h, 2)], along(axes[0], k)))

    landed(red_d)
    db_pad = s["pd"][y, c].astype(F32)
    for k in (1, 2, 3):
        db_pad = db_pad + s["rd"][k - 1].astype(F32)
    hi, lo = split(db_pad)
    dbv = mm_nt(hi, perm[...]) + mm_nt(lo, perm[...])
    gain_f_grad = jnp.sum(dbv * hidden * r2, axis=0, keepdims=True)
    ev = dbv * gain_f
    inner = jnp.mean(ev * hidden, axis=-1, keepdims=True)
    dh = cot.astype(F32) + r2 * ev - hidden * (r2 * r2 * r2 * inner)
    dh_low = dh.astype(BF16)

    def grad(tiles, value):
        for at, g in enumerate(tiles):
            s["gat"][g] = value[:, 128 * at:128 * at + 128].astype(BF16).reshape(4, 4, 4, 16, 128)

    def reduce_start(group):
        start, runs = group[0][0], sum(run[1] for run in group)
        return remote(
            s["gat"].at[pl.ds(8 * (1 - c) + start, runs)], s["gar"].at[pl.ds(start, runs)], sibling)

    def cut(axes, axis, index):
        kept = [a for a in "xzy" if a in axes]
        return tuple(index if a == axis else slice(None) for a in kept)

    def reduce_send(group, src, dst, phase):
        copies = []
        for start, runs, axes in group:
            left, axis = axes[:3 - phase], axes[2 - phase]
            first = 8 * c + start if src == "gat" else start
            for k in (1, 2, 3):
                part = s[src].at[(pl.ds(first, runs),) + cut(left, axis, (here[axis] + k) % 4)]
                copies.append(remote(part, s[dst].at[k - 1, pl.ds(start, runs)], along(axis, k)))
        return copies

    def reduce_sum(group, src, dst, phase, copies):
        landed(copies)
        for start, runs, axes in group:
            left, axis = axes[:3 - phase], axes[2 - phase]
            for t in range(start, start + runs):
                first = 8 * c + t if src == "gat" else t
                total = s[src][(first,) + cut(left, axis, here[axis])].astype(F32)
                for k in range(3):
                    total = total + s[dst][k, t].astype(F32)
                yield t, total

    def reduce_0(group, copy):
        copy.wait_recv()
        start, runs = group[0][0], sum(run[1] for run in group)
        for t in range(start, start + runs):
            s["gat"][8 * c + t] = (s["gat"][8 * c + t].astype(F32) + s["gar"][t].astype(F32)).astype(BF16)
        return reduce_send(group, "gat", "r1", 0)

    def reduce_1(group, copies):
        for t, total in reduce_sum(group, "gat", "r1", 0, copies):
            s["t2"][t] = total.astype(BF16)
        return reduce_send(group, "t2", "r2", 1)

    def reduce_2(group, copies):
        for t, total in reduce_sum(group, "t2", "r2", 1, copies):
            s["t3"][t] = total.astype(BF16)
        return reduce_send(group, "t3", "r3", 2)

    def reduce_3(group, copies):
        for t, total in reduce_sum(group, "t3", "r3", 2, copies):
            s["fin"][t] = total

    grad(OUT, mm_tn(o_pad, dh_low))
    part_o = reduce_start(REDUCE[0])
    do_pad = mm_nt(dh_low, weight(*OUT))
    do = mm_nt(do_pad.astype(BF16), pad[...]).astype(BF16)

    dk = [[None, None], [None, None]]
    dv = [[None, None], [None, None]]
    dq_tiles = []
    for t in range(7):
        if t == 1:
            part_o = reduce_0(REDUCE[0], part_o)
        if t == 2:
            fg1 = []
            for at, (src, r_1, s_1, r_2, axes) in enumerate(FG):
                for h, k in enumerate((1, 3)):
                    half[2 * at + h].wait_recv()
                    there = (here[axes[0]] + k) % 4
                    part = piece(src, axes, **{axes[0]: there, axes[1]: pl.ds(2 * h, 2)})
                    s[src][part] = (s[src][part].astype(F32) + s[r_1][2, 2 * h:2 * h + 2].astype(F32)).astype(BF16)
                    part = s[src].at[piece(src, axes, **{axes[0]: there})]
                    fg1.append(remote(part, s[r_1].at[h], along(axes[0], k)))
        do_t = do[:, 128 * t:128 * t + 128]
        total = None
        for e in range(2):
            h = 2 * t + e
            g = h // 7
            pr = s["prob"][h]
            dpr = mm_nt(do_t, values[g][e])
            ds = (pr * (dpr - jnp.sum(pr * dpr, axis=-1, keepdims=True)) * 0.125).astype(BF16)
            part = mm(ds, keys[g][e])
            total = part if total is None else total + part
            kp, vp = mm_tn(ds, q_tiles[t]), mm_tn(pr.astype(BF16), do_t)
            dk[g][e] = kp if dk[g][e] is None else dk[g][e] + kp
            dv[g][e] = vp if dv[g][e] is None else dv[g][e] + vp
        dq_tiles.append((total * cosine - swapped(total) * sine).astype(BF16))

    def gather(parts):
        lo = parts[0][0] + pltpu.roll(parts[0][1], 64, 1)
        hi = parts[1][1] + pltpu.roll(parts[1][0], 64, 1)
        return jnp.where(lane256 < 64, lo, hi)

    dkv = jnp.concatenate([gather(dk), gather(dv)], axis=1).reshape(2, T, 256)
    s["dkvf"][...] = dkv
    s["dkv"][...] = dkv.astype(BF16)
    dkv_copy = remote(s["dkv"].at[1 - yh], s["dkr"], along("y", 2))

    dq = jnp.concatenate(dq_tiles, axis=1)
    grad(QUERY, mm_tn(a_pad, dq))
    part_q = reduce_start(REDUCE[1])
    da_pad = mm_nt(dq, weight(*QUERY))
    part_q = reduce_0(REDUCE[1], part_q)
    dkv_copy.wait_recv()
    dkv_own = s["dkvf"][yh] + s["dkr"][...].astype(F32)
    dko, dvl = dkv_own[:, 0:128], dkv_own[:, 128:256].astype(BF16)
    dkl = (dko * cosine - swapped(dko) * sine).astype(BF16)
    dkvl = jnp.concatenate([dkl, dvl], axis=1)
    da_pad = da_pad + mm_nt(dkvl, weight(KEY, VALUE))
    hi, lo = split(da_pad)
    dav = mm_nt(hi, pad[...]) + mm_nt(lo, pad[...])
    gain_a_grad = jnp.sum(dav * xf * r1, axis=0, keepdims=True)
    bias_grad = jnp.sum(jnp.concatenate([dq, dkvl], axis=1).astype(F32), axis=0, keepdims=True)
    small = jnp.concatenate([gain_a_grad, gain_f_grad, bias_grad], axis=1)
    spread = (mask[...].astype(F32) * small).astype(BF16)
    small_rows = mm_nt(spread, pick[...]).astype(BF16)
    small_rows = mm_tn(last_rows, jnp.concatenate([small_rows, jnp.zeros((128, 96), BF16)], axis=1))
    kv_grad = mm_tn(a_pad, dkvl)
    grad((KEY,), kv_grad[:, 0:128] + small_rows)
    grad((VALUE,), kv_grad[:, 128:256])
    part_k = reduce_start(REDUCE[2])

    fv = dav * gain_a
    inner = jnp.mean(fv * xf, axis=-1, keepdims=True)
    store("ing", (dh + r1 * fv - xf * (r1 * r1 * r1 * inner)).astype(BF16))

    landed(fg1)
    fg2 = []
    for src, r_1, s_1, r_2, axes in FG:
        own = s[src][here["x"]] if axes[0] == "x" else s[src][:, here["z"]]
        total = own.astype(F32)
        for h in range(2):
            total = total + s[r_1][h].astype(F32)
        s[s_1][...] = total.astype(BF16)
        for k in (1, 2, 3):
            there = (here[axes[1]] + k) % 4
            fg2.append(remote(s[s_1].at[there], s[r_2].at[k - 1], along(axes[1], k)))

    part_k = reduce_0(REDUCE[2], part_k)
    part_o = reduce_1(REDUCE[0], part_o)
    landed(red_o)
    total = hidden + s["po"][y, c].astype(F32)
    for k in (1, 2, 3):
        total = total + s["ro"][k - 1].astype(F32)
    store("out", total.astype(BF16))
    part_q = reduce_1(REDUCE[1], part_q)

    landed(fg2)
    sums = []
    for src, r_1, s_1, r_2, axes in FG:
        total = s[s_1][here[axes[1]]].astype(F32)
        for k in (1, 2, 3):
            total = total + s[r_2][k - 1].astype(F32)
        sums.append(total)
    store("g_down", jnp.concatenate([sums[2][0:38], sums[3][0:38]], axis=1))
    s["wf"][0] = sums[0]
    s["wf"][1] = sums[1]
    for at in range(8):
        for g in range(2):
            s["fs"][at, g, 0:7] = s["wf"][g, 7 * at:7 * at + 7]
            s["fs"][at, g, 7:8] = jnp.zeros((1, FS), F32)
    fin_in = []
    for k in range(4):
        for e in range(2):
            if k or e:
                ty, tc = (y + k) % 4, (c + e) % 2
                fin_in.append(remote(s["fs"].at[ty * 2 + tc], s["fr"].at[me8], device(x, ty, z, tc)))
    s["fr"][me8] = s["fs"][me8]

    part_o = reduce_2(REDUCE[0], part_o)
    part_k = reduce_1(REDUCE[2], part_k)
    part_q = reduce_2(REDUCE[1], part_q)

    landed(fin_in)
    for yy in range(2):
        for xx in range(4):
            block = jnp.zeros((16, FS), F32)
            lane16 = iota((16, FS), 1)
            for q in range(4):
                moved = s["fr"][(2 * (q % 2) + yy) * 2 + q // 2].reshape(16, FS)
                if xx != q:
                    moved = pltpu.roll(moved, (160 * (q - xx)) % FS, 1)
                block = jnp.where((lane16 >= 160 * q) & (lane16 < 160 * q + 160), moved, block)
            guf[:, 2 * xx + yy] = block.reshape(2, 8, FS)
    hi, lo = split(guf[...].reshape(128, FS))
    flat = (mm_nt(hi, order[...]) + mm_nt(lo, order[...])).reshape(2, 8, 8, FS)
    for g, name in enumerate(("g_gate", "g_up")):
        for k in range(8):
            o_[name][:, 608 * k:608 * k + 608] = flat[g, k, 0:7, 0:608]
        stores[name].start()

    part_k = reduce_2(REDUCE[2], part_k)
    reduce_3(REDUCE[0], part_o)
    reduce_3(REDUCE[1], part_q)
    reduce_3(REDUCE[2], part_k)
    fin_copy = remote(s["fin"].at[:, pl.ds((1 - c) * 8, 8)], s["finr"], sibling)
    fin_copy.wait_recv()
    for t in range(8):
        own = jnp.where(c == 0, s["fin"][t, 0:8], s["fin"][t, 8:16])
        other = s["finr"][t]
        pkf[:, LANES[t]:LANES[t] + 128] = jnp.where(c == 0, own, other)
        pkf[:, LANES[8 + t]:LANES[8 + t] + 128] = jnp.where(c == 0, other, own)
    store("g_wq", pkf[0:7, 0:896])
    store("g_wk", pkf[0:7, 896:1024])
    store("g_wv", pkf[0:7, 1024:1152])
    store("g_wo", pkf[0:7, 1152:2048])
    store("g_gain_attn", pkf[7:8, 896:903])
    store("g_gain_ffn", pkf[7:8, 903:910])
    store("g_bias", pkf[7:8, 910:919])
    for copy in sends:
        copy.wait_send()
    for copy in stores.values():
        copy.wait()
    assert count[0] <= NSEM, count[0]


def hand_over(*refs):
    n = len(OUTPUTS)
    copies = [pltpu.make_async_copy(refs[k], refs[n + k], refs[2 * n].at[k]) for k in range(n)]
    for copy in copies:
        copy.start()
    for copy in copies:
        copy.wait()


def per_device(*args):
    shapes = tuple(jax.ShapeDtypeStruct(*v) for v in OUTPUTS.values())
    anywhere = pl.BlockSpec(memory_space=pl.ANY)
    results = pl.pallas_call(
        body,
        out_shape=shapes,
        in_specs=[anywhere] * len(INPUTS),
        out_specs=(anywhere,) * len(OUTPUTS),
        scratch_shapes=[
            pltpu.VMEM(shape, dtype) for part in (SCRATCH, INPUTS, OUTPUTS) for shape, dtype in part.values()]
        + [pltpu.SemaphoreType.DMA((n,)) for n in (NSEM, NSEM, len(INPUTS), len(OUTPUTS))],
        compiler_params=pltpu.CompilerParams(
            collective_id=0, has_side_effects=True, vmem_limit_bytes=60 * 2**20),
        name="layer",
    )(*(v.reshape(1, -1) if v.ndim == 1 else v for v in args))
    results = pl.pallas_call(
        hand_over,
        out_shape=shapes,
        in_specs=[anywhere] * len(OUTPUTS),
        out_specs=(pl.BlockSpec(memory_space=pltpu.VMEM),) * len(OUTPUTS),
        scratch_shapes=[pltpu.SemaphoreType.DMA((len(OUTPUTS),))],
        name="results",
    )(*results)
    return tuple(v.reshape(-1) if v.shape[0] == 1 else v for v in results)


def solution(mesh):
    both = P(("dp", "ctx"))
    rows = P(("dp", "ctx"), None)
    return jax.shard_map(
        per_device,
        mesh=mesh,
        in_specs=(rows, both, both, rows, rows, rows, both, rows, both, rows, rows, rows, rows),
        out_specs=(rows, rows, both, rows, rows, rows, both, rows, both, rows, rows, rows),
        check_vma=False,
    )
```

```python
import functools

import jax
import jax.numpy as jnp
import numpy as np
from jax import lax
from jax.experimental import pallas as pl
from jax.experimental.pallas import tpu as pltpu
from jax.sharding import PartitionSpec as P

F32 = jnp.float32
BF16 = jnp.bfloat16
MESH = pl.DeviceIdType.MESH
D = 896
DP = 1024
FF = 4864
FS = 640
T = 128
VEC = 2 * D + 1152
EPS = 1e-6
MASKED = -1e9
LANES = (0, 128, 256, 384, 896, 1280, 1408, 1536, 512, 640, 768, 1152, 1024, 1664, 1792, 1920)
QUERY, KEY, VALUE, OUT = (0, 1, 2, 3, 8, 9, 10), 4, 12, (11, 5, 6, 7, 13, 14, 15)
GATHER1 = ((0, 2, "xzy"), (2, 1, "zxy"), (3, 1, "yxz"), (4, 1, "yzx"))
GATHER2 = ((5, 1, "xzy"), (6, 1, "zxy"), (7, 1, "yxz"))
REDUCE = (((5, 1, "xzy"), (6, 1, "yxz"), (7, 1, "yzx")), ((0, 2, "xzy"), (2, 1, "yxz"), (3, 1, "yzx")), ((4, 1, "yxz"),))


def iota(shape, axis):
    return lax.broadcasted_iota(jnp.int32, shape, axis)


def sevenths(v):
    return lax.shift_right_logical(v * 9363, 16)


def ninths(v):
    return lax.shift_right_logical(v * 7282, 16)


def slot_of(i):
    return (i >> 5) * 32 + ((i >> 2) & 3) * 8 + (i & 1) * 4 + ((i >> 4) & 1) * 2 + ((i >> 1) & 1)


def one_hot(test):
    return jnp.where(test, 1.0, 0.0).astype(BF16)


def mm(a, b):
    return jnp.dot(a, b, preferred_element_type=F32)


def mm_nt(a, b):
    return lax.dot_general(a, b, (((1,), (1,)), ((), ())), preferred_element_type=F32)


def mm_tn(a, b):
    return lax.dot_general(a, b, (((0,), (0,)), ((), ())), preferred_element_type=F32)


def split(v):
    hi = v.astype(BF16)
    return hi, (v - hi.astype(F32)).astype(BF16)


INPUTS = dict(
    tok=((T, D), BF16), seg=((1, T), jnp.int32), gain_attn=((1, 7), BF16), wq=((7, D), BF16), wk=((7, 128), BF16),
    wv=((7, 128), BF16), bias_qkv=((1, 9), BF16), wo=((7, D), BF16), gain_ffn=((1, 7), BF16), wgate=((7, FF), BF16),
    wup=((7, FF), BF16), wdown=((38, D), BF16), cot=((T, D), BF16),
)
OUTPUTS = dict(
    out=((T, D), BF16), ing=((T, D), BF16), g_gain_attn=((1, 7), F32), g_wq=((7, D), F32), g_wk=((7, 128), F32),
    g_wv=((7, 128), F32), g_bias=((1, 9), F32), g_wo=((7, D), F32), g_gain_ffn=((1, 7), F32), g_gate=((7, FF), F32),
    g_up=((7, FF), F32), g_down=((38, D), F32),
)
SCRATCH = dict(
    pkf=((8, 2048), F32),
    pk=((8, 16, 128), BF16),
    pkr=((8, 16, 128), BF16),
    aw=((16, 4, 4, 4, 16, 128), BF16),
    guf=((2, 8, 8, FS), F32),
    gus=((8, 16, FS), BF16),
    gui=((8, 16, FS), BF16),
    wf=((2, 56, FS), F32),
    wg=((4, 4, 56, FS), BF16),
    wu=((4, 4, 56, FS), BF16),
    da=((4, 4, 40, 512), BF16),
    db=((4, 4, 40, 384), BF16),
    pad=((D, DP), BF16),
    perm=((D, D), BF16),
    order=((FS, FS), BF16),
    pick=((32, VEC), BF16),
    mask=((128, VEC), BF16),
    wdf=((40, D), F32),
    segs=((2, 8, 128), jnp.int32),
    kv=((2, T, 256), BF16),
    prob=((14, T, 256), F32),
    ball=((4, 2, T, D), BF16),
    yall=((4, 2, T, D), BF16),
    mb=((4, 2 * T, FS), BF16),
    dgb=((4, 2 * T, FS), BF16),
    dub=((4, 2 * T, FS), BF16),
    po=((4, 2, T, D), BF16),
    pd=((4, 2, T, D), BF16),
    qo=((4, T, D), BF16),
    qd=((4, T, D), BF16),
    ro=((3, T, D), BF16),
    rd=((3, T, D), BF16),
    gg=((4, 4, 56, FS), BF16),
    gu=((4, 4, 56, FS), BF16),
    ga=((4, 4, 40, 512), BF16),
    gb=((4, 4, 40, 384), BF16),
    rg1=((3, 4, 56, FS), BF16),
    ru1=((3, 4, 56, FS), BF16),
    ra1=((3, 4, 40, 512), BF16),
    rb1=((3, 4, 40, 384), BF16),
    sg1=((4, 56, FS), BF16),
    su1=((4, 56, FS), BF16),
    sa1=((4, 40, 512), BF16),
    sb1=((4, 40, 384), BF16),
    rg2=((3, 56, FS), BF16),
    ru2=((3, 56, FS), BF16),
    ra2=((3, 40, 512), BF16),
    rb2=((3, 40, 384), BF16),
    fs=((8, 16, FS), BF16),
    fr=((8, 16, FS), BF16),
    dkv=((2, T, 256), BF16),
    dkvf=((2, T, 256), F32),
    dkr=((T, 256), BF16),
    gat=((16, 4, 4, 4, 16, 128), BF16),
    gar=((8, 4, 4, 4, 16, 128), BF16),
    r1=((3, 8, 4, 4, 16, 128), BF16),
    t2=((8, 4, 4, 16, 128), BF16),
    r2=((3, 8, 4, 16, 128), BF16),
    t3=((8, 4, 16, 128), BF16),
    r3=((3, 8, 16, 128), BF16),
    fin=((8, 16, 128), F32),
    finr=((8, 8, 128), F32),
)
NSEM = 100


def body(*refs):
    sizes = (len(INPUTS), len(OUTPUTS), len(SCRATCH), len(INPUTS), len(OUTPUTS), 4)
    parts = []
    for size in sizes:
        parts.append(refs[sum(map(len, parts)):][:size])
    s = dict(zip(SCRATCH, parts[2]))
    i_ = dict(zip(INPUTS, parts[3]))
    o_ = dict(zip(OUTPUTS, parts[4]))
    ssem, rsem, isem, osem = parts[5]
    loads = {
        name: pltpu.make_async_copy(ref, i_[name], isem.at[n]) for n, (name, ref) in enumerate(zip(INPUTS, parts[0]))}
    stores = {
        name: pltpu.make_async_copy(o_[name], ref, osem.at[n]) for n, (name, ref) in enumerate(zip(OUTPUTS, parts[1]))}

    def load(*names):
        for name in names:
            loads[name].wait()
        return [i_[name][...] for name in names]

    def store(name, value):
        o_[name][...] = value
        stores[name].start()

    count = [0]
    di, yh = lax.axis_index("dp"), lax.axis_index("ctx")
    c, z, yl, x = di % 2, (di // 2) % 4, (di // 8) % 2, di // 16
    y = yh * 2 + yl
    here = {"x": x, "y": y, "z": z}

    def device(x, y, z, c):
        return (((x * 2 + y % 2) * 4 + z) * 2 + c, y // 2)

    def along(axis, k):
        at = dict(here)
        at[axis] = (at[axis] + k) % 4
        return device(at["x"], at["y"], at["z"], c)

    sibling = device(x, y, z, 1 - c)

    def fresh(n=1):
        count[0] += n
        return count[0] - n

    VIEWS = dict(
        tile=s["aw"].reshape(1024, 16, 128), wide=s["wg"], da=s["da"], db=s["db"], seg=s["segs"], piece=s["gui"], kv=s["kv"], rows=s["ball"].reshape(8, T, D),
        fin=s["finr"])
    groups = []

    def group(kind):
        groups.append([kind, fresh(), 0])
        return groups[-1]

    def remote(src, dst, dev, to, slots):
        copy = pltpu.make_async_remote_copy(
            src_ref=src, dst_ref=dst, send_sem=ssem.at[to[1]], recv_sem=rsem.at[to[1]],
            device_id=dev, device_id_type=MESH)
        copy.start()
        to[2] += slots

    def wait_for(sems, to):
        whole, n = VIEWS[to[0]], to[2]
        if to[0] in ("wide", "da", "db"):
            fours = {2: (1, 2), 3: (1, 3), 4: (1, 4), 6: (2, 3), 8: (2, 4)}[n]
            whole = whole.at[pl.ds(0, fours[0]), pl.ds(0, fours[1])]
        else:
            whole = whole.at[pl.ds(0, n)]
        pltpu.make_async_copy(whole, whole, sems.at[to[1]]).wait()

    def landed(*arrivals):
        for to in arrivals:
            wait_for(rsem, to)

    barrier = pltpu.get_barrier_semaphore()
    partners = [along(axis, k) for axis in "xyz" for k in (1, 2, 3)] + [sibling]
    partners += [device(x, (y + k) % 4, z, 1 - c) for k in (1, 2, 3)]
    for dev in partners:
        pl.semaphore_signal(barrier, inc=1, device_id=dev, device_id_type=MESH)

    for name in ("wgate", "wup", "wq", "wk", "wv", "wo", "gain_attn", "gain_ffn", "bias_qkv", "wdown", "seg", "cot", "tok"):
        loads[name].start()

    pad, perm, order, pick, mask = s["pad"], s["perm"], s["order"], s["pick"], s["mask"]
    r = iota((FS, 1), 0)
    u = lax.shift_right_logical(r * 1725, 16)
    target = (u & 3) * 160 + (u >> 2) * 40 + (r - u * 38)
    order[...] = one_hot((iota((FS, FS), 1) == target) & (r < 608))
    guf = s["guf"]
    guf[...] = jnp.zeros(guf.shape, F32)

    load("wgate", "wup")
    for k in range(8):
        guf[0, k, 0:7, 0:608] = i_["wgate"][:, 608 * k:608 * k + 608].astype(F32)
        guf[1, k, 0:7, 0:608] = i_["wup"][:, 608 * k:608 * k + 608].astype(F32)
    placed = mm(guf[...].reshape(128, FS).astype(BF16), order[...]).reshape(2, 4, 2, 8, FS)
    lane = iota((32, FS), 1)
    for q in range(4):
        piece = jnp.zeros((32, FS), F32)
        for xx in range(4):
            moved = placed[:, xx].reshape(32, FS)
            if xx != q:
                moved = pltpu.roll(moved, (160 * (xx - q)) % FS, 1)
            piece = jnp.where((lane >= 160 * xx) & (lane < 160 * xx + 160), moved, piece)
        piece = piece.reshape(2, 2, 8, FS)
        for yy in range(2):
            s["gus"][(2 * (q % 2) + yy) * 2 + q // 2] = jnp.concatenate(
                [piece[0, yy], piece[1, yy]], axis=0).astype(BF16)
    me8 = y * 2 + c
    s["gui"][me8] = s["gus"][me8]
    pkf = s["pkf"]
    wq, wk, wv, wo, gain_attn, gain_ffn, bias_qkv = load(
        "wq", "wk", "wv", "wo", "gain_attn", "gain_ffn", "bias_qkv")
    pkf[0:7, 0:896] = wq.astype(F32)
    pkf[0:7, 896:1024] = wk.astype(F32)
    pkf[0:7, 1024:1152] = wv.astype(F32)
    pkf[0:7, 1152:2048] = wo.astype(F32)
    pkf[7:8, :] = jnp.zeros((1, 2048), F32)
    pkf[7:8, 896:903] = gain_attn.astype(F32)
    pkf[7:8, 903:910] = gain_ffn.astype(F32)
    pkf[7:8, 910:919] = bias_qkv.astype(F32)
    for t in range(8):
        s["pk"][t] = jnp.concatenate(
            [pkf[:, at:at + 128] for at in (LANES[t], LANES[8 + t])], axis=0).astype(BF16)
    wdf = s["wdf"]
    (wdown,) = load("wdown")
    wdf[0:38] = wdown.astype(F32)
    wdf[38:40] = jnp.zeros((2, D), F32)
    s["da"][x, z] = wdf[:, 0:512].astype(BF16)
    s["db"][x, z] = wdf[:, 512:896].astype(BF16)
    (cot,) = load("cot")
    s["yall"][y, c] = cot
    (seg,) = load("seg")
    s["segs"][yh] = jnp.broadcast_to(seg, (8, 128))

    pl.semaphore_wait(barrier, len(partners))
    swap = group("tile")
    remote(s["pk"], s["pkr"], sibling, swap, 8)

    def slab(name, axes, **index):
        return s[name].at[tuple(index.get(a, here[a]) for a in "xz")]

    KIND = dict(wg="wide", wu="wide", da="da", db="db")

    def ffn_first(name, axes, to):
        part = slab(name, axes)
        for k in (1, 3, 2):
            remote(part, part, along(axes[0], k), to, 1)

    def ffn_near(name, axes):
        near = [group(KIND[name]), group(KIND[name])]
        part = slab(name, axes, **{axes[0]: slice(None)})
        for h, k in enumerate((1, 3)):
            remote(part, part, along(axes[1], k), near[h], 4)
        return near

    def ffn_far(name, axes, near):
        to = group(KIND[name])
        for h, k in enumerate((1, 3)):
            landed(near[h])
            part = slab(name, axes, **{axes[0]: pl.ds(2 * h, 2), axes[1]: (here[axes[1]] - k) % 4})
            remote(part, part, along(axes[1], k), to, 2)
        return to

    gu_in = group("piece")
    for k in (2, 1, 3, 0):
        for e in range(2):
            if k or e:
                ty, tc = (y + k) % 4, (c + e) % 2
                remote(s["gus"].at[ty * 2 + tc], s["gui"].at[me8], device(x, ty, z, tc), gu_in, 1)
    first_a, first_b, wide1 = group("da"), group("db"), group("wide")
    ffn_first("da", "xz", first_a)
    ffn_first("db", "zx", first_b)
    seg_copy = group("seg")
    remote(s["segs"].at[yh], s["segs"].at[yh], along("y", 2), seg_copy, 1)
    ring = fresh(16)
    passed = ring + 8

    def arriving(name, k):
        n = ring + k + 4 * (name == "yall")
        mine = s[name].at[y, c]
        return pltpu.make_async_remote_copy(
            src_ref=mine, dst_ref=mine, send_sem=ssem.at[n], recv_sem=rsem.at[n],
            device_id=along("y", 4 - k), device_id_type=MESH)

    def passing(name, k):
        n = passed + k + 4 * (name == "yall")
        part = s[name].at[(y + k) % 4, c]
        return pltpu.make_async_remote_copy(
            src_ref=part, dst_ref=part, send_sem=ssem.at[n], recv_sem=rsem.at[n],
            device_id=sibling, device_id_type=MESH)

    passing("yall", 0).start()
    for k in (1, 3):
        arriving("yall", k).start()

    landed(swap)
    for t in range(8):
        own, other = s["pk"][t].astype(F32), s["pkr"][t].astype(F32)
        first = jnp.concatenate([own[0:8], other[0:8]], axis=0)
        second = jnp.concatenate([other[8:16], own[8:16]], axis=0)
        s["aw"][8 * c + t, x, z, y] = jnp.where(c == 0, first, second).astype(BF16)

    def slots(name, start, runs, axes, **index):
        at = [index.get(a, slice(None) if a in axes else here[a]) for a in "xzy"]
        return s[name].at[(pl.ds(start, runs),) + tuple(at)]

    def attn_phase(tiles, phase):
        arrivals = [group("tile") for _ in range(3 if phase == 2 else 1)]
        for start, runs, axes in tiles:
            part = slots("aw", 8 * c + start, runs, axes[:phase])
            for k in (1, 2, 3):
                remote(part, part, along(axes[phase], k), arrivals[(k - 1) % len(arrivals)], runs * 4 ** phase)
        return arrivals

    first1 = attn_phase(GATHER1, 0)
    first2 = attn_phase(GATHER2, 0)
    for at in range(0, D, 128):
        d = iota((128, 1), 0) + at
        i = sevenths(d)
        pad[at:at + 128] = one_hot(iota((128, DP), 1) == slot_of(i) * 8 + (d - i * 7))
        perm[at:at + 128] = one_hot(iota((128, D), 1) == slot_of(i) * 7 + (d - i * 7))

    landed(*first1)
    second1 = attn_phase(GATHER1, 1)
    landed(*first2)
    second2 = attn_phase(GATHER2, 1)
    landed(gu_in)
    for at in range(8):
        both = s["gui"][at].astype(F32)
        s["wf"][0, 7 * at:7 * at + 7] = both[0:7]
        s["wf"][1, 7 * at:7 * at + 7] = both[8:15]
    s["wg"][x, z] = s["wf"][0].astype(BF16)
    s["wu"][x, z] = s["wf"][1].astype(BF16)
    ffn_first("wg", "xz", wide1)
    ffn_first("wu", "zx", wide1)
    landed(*second1)
    third1 = attn_phase(GATHER1, 2)
    landed(first_a, first_b)
    near_a, near_b = ffn_near("da", "xz"), ffn_near("db", "zx")
    landed(*second2)
    third2 = attn_phase(GATHER2, 2)
    landed(wide1)
    near_g, near_u = ffn_near("wg", "xz"), ffn_near("wu", "zx")

    (tok,) = load("tok")
    xf = tok.astype(F32)
    r1 = lax.rsqrt(jnp.mean(xf * xf, axis=-1, keepdims=True) + EPS)
    landed(seg_copy)
    rows0 = s["segs"][0][0:1].astype(F32)
    rows1 = s["segs"][1][0:1].astype(F32)
    own_row = jnp.where(yh == 0, rows0, rows1)
    diag = iota((T, T), 0) == iota((T, T), 1)
    own_seg = jnp.sum(jnp.where(diag, own_row, 0.0), axis=1, keepdims=True)
    length = jnp.sum(2.0 * T - jnp.sum(rows0 + rows1, axis=1, keepdims=True), axis=0, keepdims=True)
    base = (yh * T).astype(F32)
    place = iota((T, 128), 0).astype(F32) + base
    lane128 = iota((T, 128), 1)
    expo = (lane128 % 32).astype(F32) * (-2.0 / 64.0)
    freq = jnp.exp(expo * float(np.log(1e6)))
    angle = (place - own_seg * length) * freq
    cosine = jnp.cos(angle)
    low_half = lane128 % 64 < 32
    sine = jnp.where(low_half, -jnp.sin(angle), jnp.sin(angle))

    def swapped(v):
        return jnp.where(low_half, pltpu.roll(v, 96, 1), pltpu.roll(v, 32, 1))

    key_seg = jnp.concatenate([rows0, rows1], axis=1)
    key_at = iota((T, 256), 1)
    query_at = iota((T, 256), 0) + yh * T
    allowed = (key_seg == own_seg) & (key_at <= query_at)
    last_rows = one_hot(iota((128, DP), 1) == iota((128, DP), 0) * 8 + 7)
    n = iota((1, VEC), 1)
    d = jnp.where(n >= D, n - D, n)
    i = sevenths(d)
    m = n - 2 * D
    im = ninths(m)
    lane_of = jnp.where(m >= 0, 14 + m - im * 9, d - i * 7 + jnp.where(n >= D, 7, 0))
    pick[...] = one_hot(iota((32, VEC), 0) == lane_of)
    mask[...] = one_hot(iota((128, VEC), 0) == slot_of(jnp.where(m >= 0, im, i)))

    def pass_on(tiles, arrivals, between=None):
        to = group("tile")
        for start, runs, axes in tiles:
            part = slots("aw", 8 * c + start, runs, axes[:2])
            remote(part, part, sibling, to, 16 * runs)
        for k in (1, 3, 2):
            if k == 2 and between:
                between()
            landed(arrivals[k - 1])
            for start, runs, axes in tiles:
                part = slots("aw", 8 * c + start, runs, axes[:2], **{axes[2]: (here[axes[2]] - k) % 4})
                remote(part, part, sibling, to, 16 * runs)
        return to

    far = []

    def down_far():
        far.append(ffn_far("da", "xz", near_a))
        far.append(ffn_far("db", "zx", near_b))

    forward1 = pass_on(GATHER1, third1, down_far)
    far.append(ffn_far("wg", "xz", near_g))
    landed(forward1)

    def weight(*tiles):
        return jnp.concatenate([s["aw"][g].reshape(DP, 128) for g in tiles], axis=1)

    picked = mm(last_rows, weight(KEY))[:, 0:32].astype(BF16)
    vecs = jnp.sum(mm(picked, pick[...]) * mask[...].astype(F32), axis=0, keepdims=True)
    gain_a, gain_f, bias = vecs[:, 0:D], vecs[:, D:2 * D], vecs[:, 2 * D:]

    a = (xf * r1 * gain_a).astype(BF16)
    a_pad = mm(a, pad[...]).astype(BF16)
    qkv = mm(a_pad, weight(*QUERY, KEY, VALUE)) + bias

    def tile(t):
        return qkv[:, 128 * t:128 * t + 128]


    def rope(v):
        return v * cosine + swapped(v) * sine

    key_tile = rope(tile(7)).astype(BF16)
    value_tile = tile(8).astype(BF16)
    s["kv"][yh] = jnp.concatenate([key_tile, value_tile], axis=1)
    kv_copy = group("kv")
    remote(s["kv"].at[yh], s["kv"].at[yh], along("y", 2), kv_copy, 1)
    q_tiles = [rope(tile(t)).astype(BF16) for t in range(7)]

    arriving("yall", 2).start()
    far.append(ffn_far("wu", "zx", near_u))
    forward2 = pass_on(GATHER2, third2)
    landed(kv_copy)
    kv = s["kv"][...].reshape(256, 256).astype(F32)
    lane256 = iota((256, 128), 1)

    def halves(v):
        turned = pltpu.roll(v, 64, 1)
        lo, hi = lane256 < 64, lane256 >= 64
        pick2 = lambda m, u: jnp.where(m, u, 0.0).astype(BF16)
        return ((pick2(lo, v), pick2(hi, turned)), (pick2(lo, turned), pick2(hi, v)))

    keys = halves(kv[:, 0:128])
    values = halves(kv[:, 128:256])
    mixed = []
    for t in range(7):
        total = None
        for e in range(2):
            h = 2 * t + e
            logits = jnp.where(allowed, mm_nt(q_tiles[t], keys[h // 7][e]) * 0.125, MASKED)
            top = jnp.max(logits, axis=-1, keepdims=True)
            raw = jnp.exp(logits - top)
            pr = raw / jnp.sum(raw, axis=-1, keepdims=True)
            s["prob"][h] = pr
            part = mm(pr.astype(BF16), values[h // 7][e])
            total = part if total is None else total + part
        mixed.append(total.astype(BF16))
    mixed = jnp.concatenate(mixed, axis=1)
    o_pad = mm(mixed, pad[...]).astype(BF16)
    landed(forward2)
    hidden = xf + mm(o_pad, weight(*OUT))
    r2 = lax.rsqrt(jnp.mean(hidden * hidden, axis=-1, keepdims=True) + EPS)
    b = (hidden * r2 * gain_f).astype(BF16)
    s["ball"][y, c] = mm(b, perm[...]).astype(BF16)
    passing("ball", 0).start()
    for k in (1, 3):
        arriving("ball", k).start()
    landed(*far)
    base = fresh(4)
    red_d, sib_o = group("rows"), group("rows")
    red_o = [group("rows") for _ in range(4)]

    def chunk_copies(k):
        yy = (y + k) % 4
        copies = []
        for part, got, ring_in, sib, out_sem in (
                ("pd", "qd", "rd", base + k, red_d[1]), ("po", "qo", "ro", sib_o[1], red_o[0][1] + k)):
            copies.append(pltpu.make_async_remote_copy(
                src_ref=s[part].at[yy, 1 - c], dst_ref=s[got].at[yy], send_sem=ssem.at[sib], recv_sem=rsem.at[sib],
                device_id=sibling, device_id_type=MESH))
            copies.append(pltpu.make_async_remote_copy(
                src_ref=s[part].at[yy, c], dst_ref=s[ring_in].at[(k + 2) % 3], send_sem=ssem.at[out_sem],
                recv_sem=rsem.at[out_sem], device_id=along("y", k), device_id_type=MESH))
        return copies

    def turn(step):
        return step + (step // 2) * (5 - 2 * step)

    def chunk(step, carry):
        k = turn(step)
        passing("ball", k).wait_recv()
        passing("yall", k).wait_recv()
        d_sib, d_ring, o_sib, o_ring = chunk_copies(k)
        yy = (y + k) % 4
        bt = s["ball"][yy].reshape(2 * T, D)
        yt = s["yall"][yy].reshape(2 * T, D)
        gate_w, up_w = s["wg"][...].reshape(D, FS), s["wu"][...].reshape(D, FS)
        down_a, down_b = s["da"][...].reshape(FS, 512), s["db"][...].reshape(FS, 384)
        gate, up = mm(bt, gate_w), mm(bt, up_w)
        sg = 1.0 / (1.0 + jnp.exp(-gate))
        silu = gate * sg
        m = (silu * up).astype(BF16)
        dm = mm_nt(yt[:, 0:512], down_a) + mm_nt(yt[:, 512:896], down_b)
        dgate = (dm * up * sg * (1.0 + gate * (1.0 - sg))).astype(BF16)
        dup = (dm * silu).astype(BF16)
        s["mb"][yy], s["dgb"][yy], s["dub"][yy] = m, dgate, dup
        s["pd"][yy] = (mm_nt(dgate, gate_w) + mm_nt(dup, up_w)).astype(BF16).reshape(2, T, D)
        d_sib.start()
        s["po"][yy, :, :, 0:512] = mm(m, down_a).astype(BF16).reshape(2, T, 512)
        s["po"][yy, :, :, 512:896] = mm(m, down_b).astype(BF16).reshape(2, T, 384)
        o_sib.start()

        @pl.when(step == 0)
        def _():
            arriving("ball", 2).start()

        @pl.when(step < 3)
        def _():
            for name in ("yall", "ball"):
                arriving(name, turn(step + 1)).wait_recv()
                passing(name, turn(step + 1)).start()

        @pl.when(step > 0)
        def _():
            finish(turn(step - 1))

        return carry

    def finish(k):
        d_sib, d_ring, _, _ = chunk_copies(k)
        yy = (y + k) % 4
        d_sib.wait_recv()
        s["pd"][yy, c] = (s["pd"][yy, c].astype(F32) + s["qd"][yy].astype(F32)).astype(BF16)

        @pl.when(k > 0)
        def _():
            d_ring.start()

    lax.fori_loop(0, 4, chunk, 0)
    finish(turn(3))
    red_d[2], sib_o[2] = 3, 4

    FG = {"ga": ("ra1", "sa1", "ra2", "zx", "da"), "gb": ("rb1", "sb1", "rb2", "xz", "db"),
          "gg": ("rg1", "sg1", "rg2", "zx", "wide"), "gu": ("ru1", "su1", "ru2", "xz", "wide")}

    def piece(**index):
        return tuple(index.get(a, slice(None)) for a in "xz")

    def fold(src):
        r_1, _, _, axes, kind = FG[src]
        half = [group(kind), group(kind)]
        for h, k in enumerate((1, 3)):
            part = s[src].at[piece(**{axes[0]: (here[axes[0]] + 2) % 4, axes[1]: pl.ds(2 * h, 2)})]
            remote(part, s[r_1].at[2, pl.ds(2 * h, 2)], along(axes[0], k), half[h], 2)
        return half

    def spread_out(src, half):
        r_1, _, _, axes, kind = FG[src]
        to = group(kind)
        for h, k in enumerate((1, 3)):
            landed(half[h])
            there = (here[axes[0]] + k) % 4
            part = piece(**{axes[0]: there, axes[1]: pl.ds(2 * h, 2)})
            s[src][part] = (s[src][part].astype(F32) + s[r_1][2, 2 * h:2 * h + 2].astype(F32)).astype(BF16)
            remote(s[src].at[piece(**{axes[0]: there})], s[r_1].at[h], along(axes[0], k), to, 4)
        return to

    def second_axis(src, arrived):
        r_1, s_1, r_2, axes, kind = FG[src]
        landed(arrived)
        total = s[src][piece(**{axes[0]: here[axes[0]]})].astype(F32)
        for h in range(2):
            total = total + s[r_1][h].astype(F32)
        s[s_1][...] = total.astype(BF16)
        to = group(kind)
        for k in (1, 2, 3):
            remote(s[s_1].at[(here[axes[1]] + k) % 4], s[r_2].at[k - 1], along(axes[1], k), to, 1)
        return to

    def owned(src, arrived):
        _, s_1, r_2, axes, _ = FG[src]
        landed(arrived)
        total = s[s_1][here[axes[1]]].astype(F32)
        for k in range(3):
            total = total + s[r_2][k].astype(F32)
        return total

    down = mm_tn(s["mb"][...].reshape(1024, FS), s["yall"][...].reshape(1024, D))
    s["ga"][...] = down[:, 0:512].reshape(4, 4, 40, 512).astype(BF16)
    s["gb"][...] = down[:, 512:896].reshape(4, 4, 40, 384).astype(BF16)
    fg = {src: fold(src) for src in ("ga", "gb")}
    ball = s["ball"][...].reshape(1024, D)
    s["gg"][...] = mm_tn(ball, s["dgb"][...].reshape(1024, FS)).astype(BF16).reshape(4, 4, 56, FS)
    fg["gg"] = fold("gg")
    s["gu"][...] = mm_tn(ball, s["dub"][...].reshape(1024, FS)).astype(BF16).reshape(4, 4, 56, FS)
    fg["gu"] = fold("gu")
    for src in ("ga", "gb"):
        fg[src] = spread_out(src, fg[src])
    landed(sib_o)
    for k in range(4):
        yy = (y + k) % 4
        s["po"][yy, c] = (s["po"][yy, c].astype(F32) + s["qo"][yy].astype(F32)).astype(BF16)

    landed(red_d)
    for k in (1, 3):
        chunk_copies(k)[3].start()
        red_o[k][2] = 1
    db_pad = s["pd"][y, c].astype(F32)
    for k in (1, 2, 3):
        db_pad = db_pad + s["rd"][k - 1].astype(F32)
    hi, lo = split(db_pad)
    dbv = mm_nt(hi, perm[...]) + mm_nt(lo, perm[...])
    gain_f_grad = jnp.sum(dbv * hidden * r2, axis=0, keepdims=True)
    ev = dbv * gain_f
    inner = jnp.mean(ev * hidden, axis=-1, keepdims=True)
    dh = cot.astype(F32) + r2 * ev - hidden * (r2 * r2 * r2 * inner)
    dh_low = dh.astype(BF16)

    def grad(tiles, value):
        for at, g in enumerate(tiles):
            s["gat"][g] = value[:, 128 * at:128 * at + 128].astype(BF16).reshape(4, 4, 4, 16, 128)

    def reduce_start(tiles):
        start, runs = tiles[0][0], sum(run[1] for run in tiles)
        to = group("tile")
        remote(s["gat"].at[pl.ds(8 * (1 - c) + start, runs)], s["gar"].at[pl.ds(start, runs)], sibling, to, 64 * runs)
        return to

    def cut(axes, axis, index):
        kept = [a for a in "xzy" if a in axes]
        return tuple(index if a == axis else slice(None) for a in kept)

    def reduce_send(tiles, src, dst, phase):
        to = group("tile")
        for start, runs, axes in tiles:
            left, axis = axes[:3 - phase], axes[2 - phase]
            first = 8 * c + start if src == "gat" else start
            for k in (1, 2, 3):
                part = s[src].at[(pl.ds(first, runs),) + cut(left, axis, (here[axis] + k) % 4)]
                remote(part, s[dst].at[k - 1, pl.ds(start, runs)], along(axis, k), to, runs * 4 ** (2 - phase))
        return to

    def reduce_sum(tiles, src, dst, phase, arrived):
        landed(arrived)
        for start, runs, axes in tiles:
            left, axis = axes[:3 - phase], axes[2 - phase]
            for t in range(start, start + runs):
                first = 8 * c + t if src == "gat" else t
                total = s[src][(first,) + cut(left, axis, here[axis])].astype(F32)
                for k in range(3):
                    total = total + s[dst][k, t].astype(F32)
                yield t, total

    def reduce_0(tiles, arrived):
        landed(arrived)
        start, runs = tiles[0][0], sum(run[1] for run in tiles)
        for t in range(start, start + runs):
            s["gat"][8 * c + t] = (s["gat"][8 * c + t].astype(F32) + s["gar"][t].astype(F32)).astype(BF16)
        return reduce_send(tiles, "gat", "r1", 0)

    def reduce_1(tiles, arrived):
        for t, total in reduce_sum(tiles, "gat", "r1", 0, arrived):
            s["t2"][t] = total.astype(BF16)
        return reduce_send(tiles, "t2", "r2", 1)

    def reduce_2(tiles, arrived):
        for t, total in reduce_sum(tiles, "t2", "r2", 1, arrived):
            s["t3"][t] = total.astype(BF16)
        return reduce_send(tiles, "t3", "r3", 2)

    def reduce_3(tiles, arrived):
        for t, total in reduce_sum(tiles, "t3", "r3", 2, arrived):
            s["fin"][t] = total

    fg["gg"] = spread_out("gg", fg["gg"])
    grad(OUT, mm_tn(o_pad, dh_low))
    part_o = reduce_start(REDUCE[0])
    fg["gu"] = spread_out("gu", fg["gu"])
    do_pad = mm_nt(dh_low, weight(*OUT))
    do = mm_nt(do_pad.astype(BF16), pad[...]).astype(BF16)

    dk = [[None, None], [None, None]]
    dv = [[None, None], [None, None]]
    dq_tiles = []
    dsts = []
    for t in range(7):
        if t == 1:
            part_o = reduce_0(REDUCE[0], part_o)
        if t == 4:
            for src in ("ga", "gb"):
                fg[src] = second_axis(src, fg[src])
        do_t = do[:, 128 * t:128 * t + 128]
        for e in range(2):
            h = 2 * t + e
            g = h // 7
            pr = s["prob"][h]
            dpr = mm_nt(do_t, values[g][e])
            ds = (pr * (dpr - jnp.sum(pr * dpr, axis=-1, keepdims=True)) * 0.125).astype(BF16)
            dsts.append(ds)
            kp, vp = mm_tn(ds, q_tiles[t]), mm_tn(pr.astype(BF16), do_t)
            dk[g][e] = kp if dk[g][e] is None else dk[g][e] + kp
            dv[g][e] = vp if dv[g][e] is None else dv[g][e] + vp

    def gather(parts):
        lo = parts[0][0] + pltpu.roll(parts[0][1], 64, 1)
        hi = parts[1][1] + pltpu.roll(parts[1][0], 64, 1)
        return jnp.where(lane256 < 64, lo, hi)

    dkv = jnp.concatenate([gather(dk), gather(dv)], axis=1).reshape(2, T, 256)
    s["dkvf"][...] = dkv
    s["dkv"][...] = dkv.astype(BF16)
    dkv_copy = group("kv")
    remote(s["dkv"].at[1 - yh], s["dkr"], along("y", 2), dkv_copy, 1)

    for t in range(7):
        total = mm(dsts[2 * t], keys[2 * t // 7][0]) + mm(dsts[2 * t + 1], keys[(2 * t + 1) // 7][1])
        dq_tiles.append((total * cosine - swapped(total) * sine).astype(BF16))
    dq = jnp.concatenate(dq_tiles, axis=1)
    grad(QUERY, mm_tn(a_pad, dq))
    part_q = reduce_start(REDUCE[1])
    fg["gg"] = second_axis("gg", fg["gg"])
    da_pad = mm_nt(dq, weight(*QUERY))
    part_q = reduce_0(REDUCE[1], part_q)
    part_o = reduce_1(REDUCE[0], part_o)
    landed(dkv_copy)
    dkv_own = s["dkvf"][yh] + s["dkr"][...].astype(F32)
    dko, dvl = dkv_own[:, 0:128], dkv_own[:, 128:256].astype(BF16)
    dkl = (dko * cosine - swapped(dko) * sine).astype(BF16)
    dkvl = jnp.concatenate([dkl, dvl], axis=1)
    da_pad = da_pad + mm_nt(dkvl, weight(KEY, VALUE))
    hi, lo = split(da_pad)
    dav = mm_nt(hi, pad[...]) + mm_nt(lo, pad[...])
    gain_a_grad = jnp.sum(dav * xf * r1, axis=0, keepdims=True)
    bias_grad = jnp.sum(jnp.concatenate([dq, dkvl], axis=1).astype(F32), axis=0, keepdims=True)
    small = jnp.concatenate([gain_a_grad, gain_f_grad, bias_grad], axis=1)
    spread = (mask[...].astype(F32) * small).astype(BF16)
    small_rows = mm_nt(spread, pick[...]).astype(BF16)
    small_rows = mm_tn(last_rows, jnp.concatenate([small_rows, jnp.zeros((128, 96), BF16)], axis=1))
    kv_grad = mm_tn(a_pad, dkvl)
    grad((KEY,), kv_grad[:, 0:128] + small_rows)
    grad((VALUE,), kv_grad[:, 128:256])
    part_k = reduce_start(REDUCE[2])

    fv = dav * gain_a
    inner = jnp.mean(fv * xf, axis=-1, keepdims=True)
    store("ing", (dh + r1 * fv - xf * (r1 * r1 * r1 * inner)).astype(BF16))

    part_k = reduce_0(REDUCE[2], part_k)
    fg["gu"] = second_axis("gu", fg["gu"])
    part_q = reduce_1(REDUCE[1], part_q)
    part_o = reduce_2(REDUCE[0], part_o)
    part_k = reduce_1(REDUCE[2], part_k)
    chunk_copies(2)[3].start()
    red_o[2][2] = 1
    s["wf"][0] = owned("gg", fg["gg"])
    s["wf"][1] = owned("gu", fg["gu"])
    for at in range(8):
        rows = []
        for g in range(2):
            rows += [s["wf"][g, 7 * at:7 * at + 7], jnp.zeros((1, FS), F32)]
        s["fs"][at] = jnp.concatenate(rows, axis=0).astype(BF16)
    fin_in = group("piece")
    for k in range(4):
        for e in range(2):
            if k or e:
                ty, tc = (y + k) % 4, (c + e) % 2
                remote(s["fs"].at[ty * 2 + tc], s["fr"].at[me8], device(x, ty, z, tc), fin_in, 1)
    s["fr"][me8] = s["fs"][me8]
    part_k = reduce_2(REDUCE[2], part_k)
    part_q = reduce_2(REDUCE[1], part_q)
    store("g_down", jnp.concatenate([owned("ga", fg["ga"])[0:38], owned("gb", fg["gb"])[0:38]], axis=1))
    landed(*red_o[1:])
    total = hidden + s["po"][y, c].astype(F32)
    for k in range(3):
        total = total + s["ro"][k].astype(F32)
    store("out", total.astype(BF16))
    landed(fin_in)
    for yy in range(2):
        for xx in range(4):
            block = jnp.zeros((16, FS), F32)
            lane16 = iota((16, FS), 1)
            for q in range(4):
                moved = s["fr"][(2 * (q % 2) + yy) * 2 + q // 2].astype(F32)
                if xx != q:
                    moved = pltpu.roll(moved, (160 * (q - xx)) % FS, 1)
                block = jnp.where((lane16 >= 160 * q) & (lane16 < 160 * q + 160), moved, block)
            guf[:, 2 * xx + yy] = block.reshape(2, 8, FS)
    hi, lo = split(guf[...].reshape(128, FS))
    flat = (mm_nt(hi, order[...]) + mm_nt(lo, order[...])).reshape(2, 8, 8, FS)
    for g, name in enumerate(("g_gate", "g_up")):
        for k in range(8):
            o_[name][:, 608 * k:608 * k + 608] = flat[g, k, 0:7, 0:608]
        stores[name].start()

    reduce_3(REDUCE[0], part_o)
    reduce_3(REDUCE[1], part_q)
    reduce_3(REDUCE[2], part_k)
    fin_copy = group("fin")
    remote(s["fin"].at[:, pl.ds((1 - c) * 8, 8)], s["finr"], sibling, fin_copy, 8)
    landed(fin_copy)
    for t in range(8):
        own = jnp.where(c == 0, s["fin"][t, 0:8], s["fin"][t, 8:16])
        other = s["finr"][t]
        pkf[:, LANES[t]:LANES[t] + 128] = jnp.where(c == 0, own, other)
        pkf[:, LANES[8 + t]:LANES[8 + t] + 128] = jnp.where(c == 0, other, own)
    store("g_wq", pkf[0:7, 0:896])
    store("g_wk", pkf[0:7, 896:1024])
    store("g_wv", pkf[0:7, 1024:1152])
    store("g_wo", pkf[0:7, 1152:2048])
    store("g_gain_attn", pkf[7:8, 896:903])
    store("g_gain_ffn", pkf[7:8, 903:910])
    store("g_bias", pkf[7:8, 910:919])
    for k in range(4):
        chunk_copies(k)[0].wait_send()
        for name in ("ball", "yall"):
            passing(name, k).wait_send()
            if k:
                arriving(name, k).wait_send()
    for to in groups:
        if to[2]:
            wait_for(ssem, to)
    for copy in stores.values():
        copy.wait()
    assert count[0] <= NSEM, count[0]


def hand_over(*refs):
    n = len(OUTPUTS)
    copies = [pltpu.make_async_copy(refs[k], refs[n + k], refs[2 * n].at[k]) for k in range(n)]
    for copy in copies:
        copy.start()
    for copy in copies:
        copy.wait()


def per_device(*args):
    shapes = tuple(jax.ShapeDtypeStruct(*v) for v in OUTPUTS.values())
    anywhere = pl.BlockSpec(memory_space=pl.ANY)
    results = pl.pallas_call(
        body,
        out_shape=shapes,
        in_specs=[anywhere] * len(INPUTS),
        out_specs=(anywhere,) * len(OUTPUTS),
        scratch_shapes=[
            pltpu.VMEM(shape, dtype) for part in (SCRATCH, INPUTS, OUTPUTS) for shape, dtype in part.values()]
        + [pltpu.SemaphoreType.DMA((n,)) for n in (NSEM, NSEM, len(INPUTS), len(OUTPUTS))],
        compiler_params=pltpu.CompilerParams(
            collective_id=0, has_side_effects=True, vmem_limit_bytes=60 * 2**20),
        name="layer",
    )(*(v.reshape(1, -1) if v.ndim == 1 else v for v in args))
    results = pl.pallas_call(
        hand_over,
        out_shape=shapes,
        in_specs=[anywhere] * len(OUTPUTS),
        out_specs=(pl.BlockSpec(memory_space=pltpu.VMEM),) * len(OUTPUTS),
        scratch_shapes=[pltpu.SemaphoreType.DMA((len(OUTPUTS),))],
        name="results",
    )(*results)
    return tuple(v.reshape(-1) if v.shape[0] == 1 else v for v in results)


def solution(mesh):
    both = P(("dp", "ctx"))
    rows = P(("dp", "ctx"), None)
    return jax.shard_map(
        per_device,
        mesh=mesh,
        in_specs=(rows, both, both, rows, rows, rows, both, rows, both, rows, rows, rows, rows),
        out_specs=(rows, rows, both, rows, rows, rows, both, rows, both, rows, rows, rows),
        check_vma=False,
    )
```

```python
import functools

import jax
import jax.numpy as jnp
import numpy as np
from jax import lax
from jax.experimental import pallas as pl
from jax.experimental.pallas import tpu as pltpu
from jax.sharding import PartitionSpec as P

F32 = jnp.float32
BF16 = jnp.bfloat16
MESH = pl.DeviceIdType.MESH
D = 896
DP = 1024
FF = 4864
FS = 640
T = 128
VEC = 2 * D + 1152
EPS = 1e-6
MASKED = -1e9
LANES = (0, 128, 256, 384, 896, 1280, 1408, 1536, 512, 640, 768, 1152, 1024, 1664, 1792, 1920)
QUERY, KEY, VALUE, OUT = (0, 1, 2, 3, 8, 9, 10), 4, 12, (11, 5, 6, 7, 13, 14, 15)
GATHER1 = (((0, 3, "xzy"),), ((3, 1, "yxz"), (4, 1, "yzx")))
GATHER2 = (((5, 2, "xzy"),), ((7, 1, "yxz"),))
REDUCE = (((5, 1, "xzy"), (6, 1, "yxz"), (7, 1, "yzx")), ((0, 2, "xzy"), (2, 1, "yxz"), (3, 1, "yzx")), ((4, 1, "xzy"),))


def iota(shape, axis):
    return lax.broadcasted_iota(jnp.int32, shape, axis)


def sevenths(v):
    return lax.shift_right_logical(v * 9363, 16)


def ninths(v):
    return lax.shift_right_logical(v * 7282, 16)


def slot_of(i):
    return (i >> 5) * 32 + ((i >> 2) & 3) * 8 + (i & 1) * 4 + ((i >> 4) & 1) * 2 + ((i >> 1) & 1)


def one_hot(test):
    return jnp.where(test, 1.0, 0.0).astype(BF16)


def mm(a, b):
    return jnp.dot(a, b, preferred_element_type=F32)


def mm_nt(a, b):
    return lax.dot_general(a, b, (((1,), (1,)), ((), ())), preferred_element_type=F32)


def mm_tn(a, b):
    return lax.dot_general(a, b, (((0,), (0,)), ((), ())), preferred_element_type=F32)


def split(v):
    hi = v.astype(BF16)
    return hi, (v - hi.astype(F32)).astype(BF16)


INPUTS = dict(
    tok=((T, D), BF16), seg=((1, T), jnp.int32), gain_attn=((1, 7), BF16), wq=((7, D), BF16), wk=((7, 128), BF16),
    wv=((7, 128), BF16), bias_qkv=((1, 9), BF16), wo=((7, D), BF16), gain_ffn=((1, 7), BF16), wgate=((7, FF), BF16),
    wup=((7, FF), BF16), wdown=((38, D), BF16), cot=((T, D), BF16),
)
OUTPUTS = dict(
    out=((T, D), BF16), ing=((T, D), BF16), g_gain_attn=((1, 7), F32), g_wq=((7, D), F32), g_wk=((7, 128), F32),
    g_wv=((7, 128), F32), g_bias=((1, 9), F32), g_wo=((7, D), F32), g_gain_ffn=((1, 7), F32), g_gate=((7, FF), F32),
    g_up=((7, FF), F32), g_down=((38, D), F32),
)
SCRATCH = dict(
    pkf=((8, 2048), F32),
    pk=((8, 16, 128), BF16),
    pkr=((8, 16, 128), BF16),
    aw=((16, 4, 4, 4, 16, 128), BF16),
    guf=((2, 8, 8, FS), F32),
    gus=((8, 16, FS), BF16),
    gui=((8, 16, FS), BF16),
    wf=((2, 56, FS), F32),
    wg=((4, 4, 56, FS), BF16),
    wu=((4, 4, 56, FS), BF16),
    da=((4, 4, 40, 512), BF16),
    db=((4, 4, 40, 384), BF16),
    pad=((D, DP), BF16),
    perm=((D, D), BF16),
    order=((FS, FS), BF16),
    pick=((32, VEC), BF16),
    mask=((128, VEC), BF16),
    wdf=((40, D), F32),
    segs=((2, 8, 128), jnp.int32),
    kv=((2, T, 256), BF16),
    prob=((14, T, 256), F32),
    ball=((4, 2, T, D), BF16),
    yall=((4, 2, T, D), BF16),
    mb=((4, 2 * T, FS), BF16),
    dgb=((4, 2 * T, FS), BF16),
    dub=((4, 2 * T, FS), BF16),
    po=((4, 2, T, D), BF16),
    pd=((4, 2, T, D), BF16),
    qo=((4, T, D), BF16),
    qd=((4, T, D), BF16),
    ro=((3, T, D), BF16),
    rd=((3, T, D), BF16),
    gg=((4, 4, 56, FS), BF16),
    gu=((4, 4, 56, FS), BF16),
    ga=((4, 4, 40, 512), BF16),
    gb=((4, 4, 40, 384), BF16),
    rg1=((3, 4, 56, FS), BF16),
    ru1=((3, 4, 56, FS), BF16),
    ra1=((3, 4, 40, 512), BF16),
    rb1=((3, 4, 40, 384), BF16),
    sg1=((4, 56, FS), BF16),
    su1=((4, 56, FS), BF16),
    sa1=((4, 40, 512), BF16),
    sb1=((4, 40, 384), BF16),
    rg2=((3, 56, FS), BF16),
    ru2=((3, 56, FS), BF16),
    ra2=((3, 40, 512), BF16),
    rb2=((3, 40, 384), BF16),
    fs=((8, 16, FS), BF16),
    fr=((8, 16, FS), BF16),
    dkv=((2, T, 256), BF16),
    dkvf=((2, T, 256), F32),
    dkr=((T, 256), BF16),
    gat=((16, 4, 4, 4, 16, 128), BF16),
    gar=((8, 4, 4, 4, 16, 128), BF16),
    r1=((3, 8, 4, 4, 16, 128), BF16),
    t2=((8, 4, 4, 16, 128), BF16),
    r2=((3, 8, 4, 16, 128), BF16),
    t3=((8, 4, 16, 128), BF16),
    r3=((3, 8, 16, 128), BF16),
    rp=((15, 16, 128), BF16),
    fin=((8, 16, 128), F32),
    finr=((8, 8, 128), F32),
)
NSEM = 100


def body(*refs):
    sizes = (len(INPUTS), len(OUTPUTS), len(SCRATCH), len(INPUTS), len(OUTPUTS), 4)
    parts = []
    for size in sizes:
        parts.append(refs[sum(map(len, parts)):][:size])
    s = dict(zip(SCRATCH, parts[2]))
    i_ = dict(zip(INPUTS, parts[3]))
    o_ = dict(zip(OUTPUTS, parts[4]))
    ssem, rsem, isem, osem = parts[5]
    loads = {
        name: pltpu.make_async_copy(ref, i_[name], isem.at[n]) for n, (name, ref) in enumerate(zip(INPUTS, parts[0]))}
    stores = {
        name: pltpu.make_async_copy(o_[name], ref, osem.at[n]) for n, (name, ref) in enumerate(zip(OUTPUTS, parts[1]))}

    def load(*names):
        for name in names:
            loads[name].wait()
        return [i_[name][...] for name in names]

    def store(name, value):
        o_[name][...] = value
        stores[name].start()

    count = [0]
    di, yh = lax.axis_index("dp"), lax.axis_index("ctx")
    c, z, yl, x = di % 2, (di // 2) % 4, (di // 8) % 2, di // 16
    y = yh * 2 + yl
    here = {"x": x, "y": y, "z": z}

    def device(x, y, z, c):
        return (((x * 2 + y % 2) * 4 + z) * 2 + c, y // 2)

    def along(axis, k):
        at = dict(here)
        at[axis] = (at[axis] + k) % 4
        return device(at["x"], at["y"], at["z"], c)

    sibling = device(x, y, z, 1 - c)

    def fresh(n=1):
        count[0] += n
        return count[0] - n

    VIEWS = dict(
        tile=s["aw"].reshape(1024, 16, 128), wide=s["wg"], da=s["da"], db=s["db"], seg=s["segs"], piece=s["gui"], kv=s["kv"], rows=s["ball"].reshape(8, T, D),
        fin=s["finr"])
    groups = []

    def group(kind):
        groups.append([kind, fresh(), 0])
        return groups[-1]

    def remote(src, dst, dev, to, slots):
        copy = pltpu.make_async_remote_copy(
            src_ref=src, dst_ref=dst, send_sem=ssem.at[to[1]], recv_sem=rsem.at[to[1]],
            device_id=dev, device_id_type=MESH)
        copy.start()
        to[2] += slots

    def wait_for(sems, to):
        whole, n = VIEWS[to[0]], to[2]
        if to[0] in ("wide", "da", "db"):
            fours = {2: (1, 2), 3: (1, 3), 4: (1, 4), 6: (2, 3), 8: (2, 4)}[n]
            whole = whole.at[pl.ds(0, fours[0]), pl.ds(0, fours[1])]
        else:
            whole = whole.at[pl.ds(0, n)]
        pltpu.make_async_copy(whole, whole, sems.at[to[1]]).wait()

    def landed(*arrivals):
        for to in arrivals:
            wait_for(rsem, to)

    barrier = pltpu.get_barrier_semaphore()
    partners = [along(axis, k) for axis in "xyz" for k in (1, 2, 3)] + [sibling]
    partners += [device(x, (y + k) % 4, z, 1 - c) for k in (1, 2, 3)]
    plane = [(i, j) for i in range(4) for j in range(4) if i or j]
    partners += [device((x + i) % 4, y, (z + j) % 4, c) for i, j in plane if i and j]
    for dev in partners:
        pl.semaphore_signal(barrier, inc=1, device_id=dev, device_id_type=MESH)

    for name in ("wgate", "wup", "wq", "wk", "wv", "wo", "gain_attn", "gain_ffn", "bias_qkv", "wdown", "seg", "cot", "tok"):
        loads[name].start()

    pad, perm, order, pick, mask = s["pad"], s["perm"], s["order"], s["pick"], s["mask"]
    r = iota((FS, 1), 0)
    u = lax.shift_right_logical(r * 1725, 16)
    target = (u & 3) * 160 + (u >> 2) * 40 + (r - u * 38)
    order[...] = one_hot((iota((FS, FS), 1) == target) & (r < 608))
    guf = s["guf"]
    guf[...] = jnp.zeros(guf.shape, F32)

    load("wgate", "wup")
    for k in range(8):
        guf[0, k, 0:7, 0:608] = i_["wgate"][:, 608 * k:608 * k + 608].astype(F32)
        guf[1, k, 0:7, 0:608] = i_["wup"][:, 608 * k:608 * k + 608].astype(F32)
    placed = mm(guf[...].reshape(128, FS).astype(BF16), order[...]).reshape(2, 4, 2, 8, FS)
    lane = iota((32, FS), 1)
    for q in range(4):
        piece = jnp.zeros((32, FS), F32)
        for xx in range(4):
            moved = placed[:, xx].reshape(32, FS)
            if xx != q:
                moved = pltpu.roll(moved, (160 * (xx - q)) % FS, 1)
            piece = jnp.where((lane >= 160 * xx) & (lane < 160 * xx + 160), moved, piece)
        piece = piece.reshape(2, 2, 8, FS)
        for yy in range(2):
            s["gus"][(2 * (q % 2) + yy) * 2 + q // 2] = jnp.concatenate(
                [piece[0, yy], piece[1, yy]], axis=0).astype(BF16)
    me8 = y * 2 + c
    s["gui"][me8] = s["gus"][me8]
    pkf = s["pkf"]
    wq, wk, wv, wo, gain_attn, gain_ffn, bias_qkv = load(
        "wq", "wk", "wv", "wo", "gain_attn", "gain_ffn", "bias_qkv")
    pkf[0:7, 0:896] = wq.astype(F32)
    pkf[0:7, 896:1024] = wk.astype(F32)
    pkf[0:7, 1024:1152] = wv.astype(F32)
    pkf[0:7, 1152:2048] = wo.astype(F32)
    pkf[7:8, :] = jnp.zeros((1, 2048), F32)
    pkf[7:8, 896:903] = gain_attn.astype(F32)
    pkf[7:8, 903:910] = gain_ffn.astype(F32)
    pkf[7:8, 910:919] = bias_qkv.astype(F32)
    for t in range(8):
        s["pk"][t] = jnp.concatenate(
            [pkf[:, at:at + 128] for at in (LANES[t], LANES[8 + t])], axis=0).astype(BF16)
    wdf = s["wdf"]
    (wdown,) = load("wdown")
    wdf[0:38] = wdown.astype(F32)
    wdf[38:40] = jnp.zeros((2, D), F32)
    s["da"][x, z] = wdf[:, 0:512].astype(BF16)
    s["db"][x, z] = wdf[:, 512:896].astype(BF16)
    (cot,) = load("cot")
    s["yall"][y, c] = cot
    (seg,) = load("seg")
    s["segs"][yh] = jnp.broadcast_to(seg, (8, 128))

    pl.semaphore_wait(barrier, len(partners))
    swap = group("tile")
    remote(s["pk"], s["pkr"], sibling, swap, 8)

    def slab(name, axes, **index):
        return s[name].at[tuple(index.get(a, here[a]) for a in "xz")]

    KIND = dict(wg="wide", wu="wide", da="da", db="db")

    def ffn_first(name, axes, to):
        part = slab(name, axes)
        for k in (1, 3, 2):
            remote(part, part, along(axes[0], k), to, 1)

    def ffn_near(name, axes):
        near = [group(KIND[name]), group(KIND[name])]
        part = slab(name, axes, **{axes[0]: slice(None)})
        for h, k in enumerate((1, 3)):
            remote(part, part, along(axes[1], k), near[h], 4)
        return near

    def ffn_far(name, axes, near):
        to = group(KIND[name])
        for h, k in enumerate((1, 3)):
            landed(near[h])
            part = slab(name, axes, **{axes[0]: pl.ds(2 * h, 2), axes[1]: (here[axes[1]] - k) % 4})
            remote(part, part, along(axes[1], k), to, 2)
        return to

    gu_in = group("piece")
    for k in (2, 1, 3, 0):
        for e in range(2):
            if k or e:
                ty, tc = (y + k) % 4, (c + e) % 2
                remote(s["gus"].at[ty * 2 + tc], s["gui"].at[me8], device(x, ty, z, tc), gu_in, 1)
    first_a, first_b, wide1 = group("da"), group("db"), group("wide")
    ffn_first("da", "xz", first_a)
    ffn_first("db", "zx", first_b)
    seg_copy = group("seg")
    remote(s["segs"].at[yh], s["segs"].at[yh], along("y", 2), seg_copy, 1)
    ring = fresh(16)
    passed = ring + 8

    def arriving(name, k):
        n = ring + k + 4 * (name == "yall")
        mine = s[name].at[y, c]
        return pltpu.make_async_remote_copy(
            src_ref=mine, dst_ref=mine, send_sem=ssem.at[n], recv_sem=rsem.at[n],
            device_id=along("y", 4 - k), device_id_type=MESH)

    def passing(name, k):
        n = passed + k + 4 * (name == "yall")
        part = s[name].at[(y + k) % 4, c]
        return pltpu.make_async_remote_copy(
            src_ref=part, dst_ref=part, send_sem=ssem.at[n], recv_sem=rsem.at[n],
            device_id=sibling, device_id_type=MESH)

    passing("yall", 0).start()
    for k in (1, 3):
        arriving("yall", k).start()

    landed(swap)
    for t in range(8):
        own, other = s["pk"][t].astype(F32), s["pkr"][t].astype(F32)
        first = jnp.concatenate([own[0:8], other[0:8]], axis=0)
        second = jnp.concatenate([other[8:16], own[8:16]], axis=0)
        s["aw"][8 * c + t, x, z, y] = jnp.where(c == 0, first, second).astype(BF16)

    def slots(name, start, runs, axes, **index):
        at = [index.get(a, slice(None) if a in axes else here[a]) for a in "xzy"]
        return s[name].at[(pl.ds(start, runs),) + tuple(at)]

    def attn_phase(tiles, phase):
        arrivals = [group("tile") for _ in range(3 if phase == 2 else 1)]
        for start, runs, axes in tiles:
            part = slots("aw", 8 * c + start, runs, axes[:phase])
            for k in (1, 2, 3):
                remote(part, part, along(axes[phase], k), arrivals[(k - 1) % len(arrivals)], runs * 4 ** phase)
        return arrivals

    def attn_plane(tiles):
        to = group("tile")
        for start, runs, axes in tiles:
            part = slots("aw", 8 * c + start, runs, "")
            for i, j in plane:
                remote(part, part, device((x + i) % 4, y, (z + j) % 4, c), to, runs)
        return to

    plane1 = attn_plane(GATHER1[0])
    first1 = attn_phase(GATHER1[1], 0)
    plane2 = attn_plane(GATHER2[0])
    first2 = attn_phase(GATHER2[1], 0)
    for at in range(0, D, 128):
        d = iota((128, 1), 0) + at
        i = sevenths(d)
        pad[at:at + 128] = one_hot(iota((128, DP), 1) == slot_of(i) * 8 + (d - i * 7))
        perm[at:at + 128] = one_hot(iota((128, D), 1) == slot_of(i) * 7 + (d - i * 7))

    landed(*first1)
    second1 = attn_phase(GATHER1[1], 1)
    landed(plane1)
    third1y = attn_phase(GATHER1[0], 2)
    landed(*first2)
    second2 = attn_phase(GATHER2[1], 1)
    landed(gu_in)
    for at in range(8):
        both = s["gui"][at].astype(F32)
        s["wf"][0, 7 * at:7 * at + 7] = both[0:7]
        s["wf"][1, 7 * at:7 * at + 7] = both[8:15]
    s["wg"][x, z] = s["wf"][0].astype(BF16)
    s["wu"][x, z] = s["wf"][1].astype(BF16)
    ffn_first("wg", "xz", wide1)
    ffn_first("wu", "zx", wide1)
    landed(*second1)
    third1 = attn_phase(GATHER1[1], 2)
    landed(first_a, first_b)
    near_a, near_b = ffn_near("da", "xz"), ffn_near("db", "zx")
    landed(*second2)
    third2 = attn_phase(GATHER2[1], 2)
    landed(plane2)
    third2y = attn_phase(GATHER2[0], 2)
    landed(wide1)
    near_g, near_u = ffn_near("wg", "xz"), ffn_near("wu", "zx")

    (tok,) = load("tok")
    xf = tok.astype(F32)
    r1 = lax.rsqrt(jnp.mean(xf * xf, axis=-1, keepdims=True) + EPS)
    landed(seg_copy)
    rows0 = s["segs"][0][0:1].astype(F32)
    rows1 = s["segs"][1][0:1].astype(F32)
    own_row = jnp.where(yh == 0, rows0, rows1)
    diag = iota((T, T), 0) == iota((T, T), 1)
    own_seg = jnp.sum(jnp.where(diag, own_row, 0.0), axis=1, keepdims=True)
    length = jnp.sum(2.0 * T - jnp.sum(rows0 + rows1, axis=1, keepdims=True), axis=0, keepdims=True)
    base = (yh * T).astype(F32)
    place = iota((T, 128), 0).astype(F32) + base
    lane128 = iota((T, 128), 1)
    expo = (lane128 % 32).astype(F32) * (-2.0 / 64.0)
    freq = jnp.exp(expo * float(np.log(1e6)))
    angle = (place - own_seg * length) * freq
    cosine = jnp.cos(angle)
    low_half = lane128 % 64 < 32
    sine = jnp.where(low_half, -jnp.sin(angle), jnp.sin(angle))

    def swapped(v):
        return jnp.where(low_half, pltpu.roll(v, 96, 1), pltpu.roll(v, 32, 1))

    key_seg = jnp.concatenate([rows0, rows1], axis=1)
    key_at = iota((T, 256), 1)
    query_at = iota((T, 256), 0) + yh * T
    allowed = (key_seg == own_seg) & (key_at <= query_at)
    last_rows = one_hot(iota((128, DP), 1) == iota((128, DP), 0) * 8 + 7)
    n = iota((1, VEC), 1)
    d = jnp.where(n >= D, n - D, n)
    i = sevenths(d)
    m = n - 2 * D
    im = ninths(m)
    lane_of = jnp.where(m >= 0, 14 + m - im * 9, d - i * 7 + jnp.where(n >= D, 7, 0))
    pick[...] = one_hot(iota((32, VEC), 0) == lane_of)
    mask[...] = one_hot(iota((128, VEC), 0) == slot_of(jnp.where(m >= 0, im, i)))

    def pass_on(tiles, arrivals, between=None):
        to = group("tile")
        for start, runs, axes in tiles:
            part = slots("aw", 8 * c + start, runs, axes[:2])
            remote(part, part, sibling, to, 16 * runs)
        for k in (1, 3, 2):
            if k == 2 and between:
                between()
            landed(arrivals[k - 1])
            for start, runs, axes in tiles:
                part = slots("aw", 8 * c + start, runs, axes[:2], **{axes[2]: (here[axes[2]] - k) % 4})
                remote(part, part, sibling, to, 16 * runs)
        return to

    far = []

    def down_far():
        far.append(ffn_far("da", "xz", near_a))
        far.append(ffn_far("db", "zx", near_b))

    forward1 = [pass_on(GATHER1[1], third1), pass_on(GATHER1[0], third1y, down_far)]
    far.append(ffn_far("wg", "xz", near_g))
    landed(*forward1)

    def weight(*tiles):
        return jnp.concatenate([s["aw"][g].reshape(DP, 128) for g in tiles], axis=1)

    picked = mm(last_rows, weight(KEY))[:, 0:32].astype(BF16)
    vecs = jnp.sum(mm(picked, pick[...]) * mask[...].astype(F32), axis=0, keepdims=True)
    gain_a, gain_f, bias = vecs[:, 0:D], vecs[:, D:2 * D], vecs[:, 2 * D:]

    a = (xf * r1 * gain_a).astype(BF16)
    a_pad = mm(a, pad[...]).astype(BF16)
    qkv = mm(a_pad, weight(*QUERY, KEY, VALUE)) + bias

    def tile(t):
        return qkv[:, 128 * t:128 * t + 128]


    def rope(v):
        return v * cosine + swapped(v) * sine

    key_tile = rope(tile(7)).astype(BF16)
    value_tile = tile(8).astype(BF16)
    s["kv"][yh] = jnp.concatenate([key_tile, value_tile], axis=1)
    kv_copy = group("kv")
    remote(s["kv"].at[yh], s["kv"].at[yh], along("y", 2), kv_copy, 1)
    q_tiles = [rope(tile(t)).astype(BF16) for t in range(7)]

    arriving("yall", 2).start()
    far.append(ffn_far("wu", "zx", near_u))
    forward2 = [pass_on(GATHER2[1], third2), pass_on(GATHER2[0], third2y)]
    landed(kv_copy)
    kv = s["kv"][...].reshape(256, 256).astype(F32)
    lane256 = iota((256, 128), 1)

    def halves(v):
        turned = pltpu.roll(v, 64, 1)
        lo, hi = lane256 < 64, lane256 >= 64
        pick2 = lambda m, u: jnp.where(m, u, 0.0).astype(BF16)
        return ((pick2(lo, v), pick2(hi, turned)), (pick2(lo, turned), pick2(hi, v)))

    keys = halves(kv[:, 0:128])
    values = halves(kv[:, 128:256])
    mixed = []
    for t in range(7):
        total = None
        for e in range(2):
            h = 2 * t + e
            logits = jnp.where(allowed, mm_nt(q_tiles[t], keys[h // 7][e]) * 0.125, MASKED)
            top = jnp.max(logits, axis=-1, keepdims=True)
            raw = jnp.exp(logits - top)
            pr = raw / jnp.sum(raw, axis=-1, keepdims=True)
            s["prob"][h] = pr
            part = mm(pr.astype(BF16), values[h // 7][e])
            total = part if total is None else total + part
        mixed.append(total.astype(BF16))
    mixed = jnp.concatenate(mixed, axis=1)
    o_pad = mm(mixed, pad[...]).astype(BF16)
    landed(*forward2)
    hidden = xf + mm(o_pad, weight(*OUT))
    r2 = lax.rsqrt(jnp.mean(hidden * hidden, axis=-1, keepdims=True) + EPS)
    b = (hidden * r2 * gain_f).astype(BF16)
    s["ball"][y, c] = mm(b, perm[...]).astype(BF16)
    passing("ball", 0).start()
    for k in (1, 3):
        arriving("ball", k).start()
    landed(*far)
    base = fresh(4)
    red_d, sib_o = group("rows"), group("rows")
    red_o = [group("rows") for _ in range(4)]

    def chunk_copies(k):
        yy = (y + k) % 4
        copies = []
        for part, got, ring_in, sib, out_sem in (
                ("pd", "qd", "rd", base + k, red_d[1]), ("po", "qo", "ro", sib_o[1], red_o[0][1] + k)):
            copies.append(pltpu.make_async_remote_copy(
                src_ref=s[part].at[yy, 1 - c], dst_ref=s[got].at[yy], send_sem=ssem.at[sib], recv_sem=rsem.at[sib],
                device_id=sibling, device_id_type=MESH))
            copies.append(pltpu.make_async_remote_copy(
                src_ref=s[part].at[yy, c], dst_ref=s[ring_in].at[(k + 2) % 3], send_sem=ssem.at[out_sem],
                recv_sem=rsem.at[out_sem], device_id=along("y", k), device_id_type=MESH))
        return copies

    def turn(step):
        return step + (step // 2) * (5 - 2 * step)

    def chunk(step, carry):
        k = turn(step)
        passing("ball", k).wait_recv()
        passing("yall", k).wait_recv()
        d_sib, d_ring, o_sib, o_ring = chunk_copies(k)
        yy = (y + k) % 4
        bt = s["ball"][yy].reshape(2 * T, D)
        yt = s["yall"][yy].reshape(2 * T, D)
        gate_w, up_w = s["wg"][...].reshape(D, FS), s["wu"][...].reshape(D, FS)
        down_a, down_b = s["da"][...].reshape(FS, 512), s["db"][...].reshape(FS, 384)
        gate, up = mm(bt, gate_w), mm(bt, up_w)
        sg = 1.0 / (1.0 + jnp.exp(-gate))
        silu = gate * sg
        m = (silu * up).astype(BF16)
        dm = mm_nt(yt[:, 0:512], down_a) + mm_nt(yt[:, 512:896], down_b)
        dgate = (dm * up * sg * (1.0 + gate * (1.0 - sg))).astype(BF16)
        dup = (dm * silu).astype(BF16)
        s["mb"][yy], s["dgb"][yy], s["dub"][yy] = m, dgate, dup
        s["pd"][yy] = (mm_nt(dgate, gate_w) + mm_nt(dup, up_w)).astype(BF16).reshape(2, T, D)
        d_sib.start()
        s["po"][yy, :, :, 0:512] = mm(m, down_a).astype(BF16).reshape(2, T, 512)
        s["po"][yy, :, :, 512:896] = mm(m, down_b).astype(BF16).reshape(2, T, 384)
        o_sib.start()

        @pl.when(step == 0)
        def _():
            arriving("ball", 2).start()

        @pl.when(step < 3)
        def _():
            for name in ("yall", "ball"):
                arriving(name, turn(step + 1)).wait_recv()
                passing(name, turn(step + 1)).start()

        @pl.when(step > 0)
        def _():
            finish(turn(step - 1))

        return carry

    def finish(k):
        d_sib, d_ring, _, _ = chunk_copies(k)
        yy = (y + k) % 4
        d_sib.wait_recv()
        s["pd"][yy, c] = (s["pd"][yy, c].astype(F32) + s["qd"][yy].astype(F32)).astype(BF16)

        @pl.when(k > 0)
        def _():
            d_ring.start()

    lax.fori_loop(0, 4, chunk, 0)
    finish(turn(3))
    red_d[2], sib_o[2] = 3, 4

    FG = {"ga": ("ra1", "sa1", "ra2", "zx", "da"), "gb": ("rb1", "sb1", "rb2", "xz", "db"),
          "gg": ("rg1", "sg1", "rg2", "zx", "wide"), "gu": ("ru1", "su1", "ru2", "xz", "wide")}

    def piece(**index):
        return tuple(index.get(a, slice(None)) for a in "xz")

    def fold(src):
        r_1, _, _, axes, kind = FG[src]
        half = [group(kind), group(kind)]
        for h, k in enumerate((1, 3)):
            part = s[src].at[piece(**{axes[0]: (here[axes[0]] + 2) % 4, axes[1]: pl.ds(2 * h, 2)})]
            remote(part, s[r_1].at[2, pl.ds(2 * h, 2)], along(axes[0], k), half[h], 2)
        return half

    def spread_out(src, half):
        r_1, _, _, axes, kind = FG[src]
        to = group(kind)
        for h, k in enumerate((1, 3)):
            landed(half[h])
            there = (here[axes[0]] + k) % 4
            part = piece(**{axes[0]: there, axes[1]: pl.ds(2 * h, 2)})
            s[src][part] = (s[src][part].astype(F32) + s[r_1][2, 2 * h:2 * h + 2].astype(F32)).astype(BF16)
            remote(s[src].at[piece(**{axes[0]: there})], s[r_1].at[h], along(axes[0], k), to, 4)
        return to

    def second_axis(src, arrived):
        r_1, s_1, r_2, axes, kind = FG[src]
        landed(arrived)
        total = s[src][piece(**{axes[0]: here[axes[0]]})].astype(F32)
        for h in range(2):
            total = total + s[r_1][h].astype(F32)
        s[s_1][...] = total.astype(BF16)
        to = group(kind)
        for k in (1, 2, 3):
            remote(s[s_1].at[(here[axes[1]] + k) % 4], s[r_2].at[k - 1], along(axes[1], k), to, 1)
        return to

    def owned(src, arrived):
        _, s_1, r_2, axes, _ = FG[src]
        landed(arrived)
        total = s[s_1][here[axes[1]]].astype(F32)
        for k in range(3):
            total = total + s[r_2][k].astype(F32)
        return total

    down = mm_tn(s["mb"][...].reshape(1024, FS), s["yall"][...].reshape(1024, D))
    s["ga"][...] = down[:, 0:512].reshape(4, 4, 40, 512).astype(BF16)
    s["gb"][...] = down[:, 512:896].reshape(4, 4, 40, 384).astype(BF16)
    fg = {src: fold(src) for src in ("ga", "gb")}
    ball = s["ball"][...].reshape(1024, D)
    s["gg"][...] = mm_tn(ball, s["dgb"][...].reshape(1024, FS)).astype(BF16).reshape(4, 4, 56, FS)
    fg["gg"] = fold("gg")
    s["gu"][...] = mm_tn(ball, s["dub"][...].reshape(1024, FS)).astype(BF16).reshape(4, 4, 56, FS)
    fg["gu"] = fold("gu")
    for src in ("ga", "gb"):
        fg[src] = spread_out(src, fg[src])
    landed(sib_o)
    for k in range(4):
        yy = (y + k) % 4
        s["po"][yy, c] = (s["po"][yy, c].astype(F32) + s["qo"][yy].astype(F32)).astype(BF16)

    landed(red_d)
    for k in (1, 3):
        chunk_copies(k)[3].start()
        red_o[k][2] = 1
    db_pad = s["pd"][y, c].astype(F32)
    for k in (1, 2, 3):
        db_pad = db_pad + s["rd"][k - 1].astype(F32)
    hi, lo = split(db_pad)
    dbv = mm_nt(hi, perm[...]) + mm_nt(lo, perm[...])
    gain_f_grad = jnp.sum(dbv * hidden * r2, axis=0, keepdims=True)
    ev = dbv * gain_f
    inner = jnp.mean(ev * hidden, axis=-1, keepdims=True)
    dh = cot.astype(F32) + r2 * ev - hidden * (r2 * r2 * r2 * inner)
    dh_low = dh.astype(BF16)

    def grad(tiles, value):
        for at, g in enumerate(tiles):
            s["gat"][g] = value[:, 128 * at:128 * at + 128].astype(BF16).reshape(4, 4, 4, 16, 128)

    def reduce_start(tiles):
        start, runs = tiles[0][0], sum(run[1] for run in tiles)
        to = group("tile")
        remote(s["gat"].at[pl.ds(8 * (1 - c) + start, runs)], s["gar"].at[pl.ds(start, runs)], sibling, to, 64 * runs)
        return to

    def cut(axes, axis, index):
        kept = [a for a in "xzy" if a in axes]
        return tuple(index if a == axis else slice(None) for a in kept)

    def reduce_send(tiles, src, dst, phase):
        to = group("tile")
        for start, runs, axes in tiles:
            left, axis = axes[:3 - phase], axes[2 - phase]
            first = 8 * c + start if src == "gat" else start
            for k in (1, 2, 3):
                part = s[src].at[(pl.ds(first, runs),) + cut(left, axis, (here[axis] + k) % 4)]
                remote(part, s[dst].at[k - 1, pl.ds(start, runs)], along(axis, k), to, runs * 4 ** (2 - phase))
        return to

    def reduce_sum(tiles, src, dst, phase, arrived):
        landed(arrived)
        for start, runs, axes in tiles:
            left, axis = axes[:3 - phase], axes[2 - phase]
            for t in range(start, start + runs):
                first = 8 * c + t if src == "gat" else t
                total = s[src][(first,) + cut(left, axis, here[axis])].astype(F32)
                for k in range(3):
                    total = total + s[dst][k, t].astype(F32)
                yield t, total

    def reduce_0(tiles, arrived):
        landed(arrived)
        start, runs = tiles[0][0], sum(run[1] for run in tiles)
        for t in range(start, start + runs):
            s["gat"][8 * c + t] = (s["gat"][8 * c + t].astype(F32) + s["gar"][t].astype(F32)).astype(BF16)
        return reduce_send(tiles, "gat", "r1", 0)

    def reduce_1(tiles, arrived):
        for t, total in reduce_sum(tiles, "gat", "r1", 0, arrived):
            s["t2"][t] = total.astype(BF16)
        return reduce_send(tiles, "t2", "r2", 1)

    def reduce_2(tiles, arrived):
        for t, total in reduce_sum(tiles, "t2", "r2", 1, arrived):
            s["t3"][t] = total.astype(BF16)
        return reduce_send(tiles, "t3", "r3", 2)

    def reduce_3(tiles, arrived):
        for t, total in reduce_sum(tiles, "t3", "r3", 2, arrived):
            s["fin"][t] = total

    fg["gg"] = spread_out("gg", fg["gg"])
    grad(OUT, mm_tn(o_pad, dh_low))
    part_o = reduce_start(REDUCE[0])
    fg["gu"] = spread_out("gu", fg["gu"])
    do_pad = mm_nt(dh_low, weight(*OUT))
    do = mm_nt(do_pad.astype(BF16), pad[...]).astype(BF16)

    dk = [[None, None], [None, None]]
    dv = [[None, None], [None, None]]
    dq_tiles = []
    dsts = []
    for t in range(7):
        if t == 1:
            part_o = reduce_0(REDUCE[0], part_o)
        if t == 4:
            for src in ("ga", "gb"):
                fg[src] = second_axis(src, fg[src])
        do_t = do[:, 128 * t:128 * t + 128]
        for e in range(2):
            h = 2 * t + e
            g = h // 7
            pr = s["prob"][h]
            dpr = mm_nt(do_t, values[g][e])
            ds = (pr * (dpr - jnp.sum(pr * dpr, axis=-1, keepdims=True)) * 0.125).astype(BF16)
            dsts.append(ds)
            kp, vp = mm_tn(ds, q_tiles[t]), mm_tn(pr.astype(BF16), do_t)
            dk[g][e] = kp if dk[g][e] is None else dk[g][e] + kp
            dv[g][e] = vp if dv[g][e] is None else dv[g][e] + vp

    def gather(parts):
        lo = parts[0][0] + pltpu.roll(parts[0][1], 64, 1)
        hi = parts[1][1] + pltpu.roll(parts[1][0], 64, 1)
        return jnp.where(lane256 < 64, lo, hi)

    dkv = jnp.concatenate([gather(dk), gather(dv)], axis=1).reshape(2, T, 256)
    s["dkvf"][...] = dkv
    s["dkv"][...] = dkv.astype(BF16)
    dkv_copy = group("kv")
    remote(s["dkv"].at[1 - yh], s["dkr"], along("y", 2), dkv_copy, 1)

    for t in range(7):
        total = mm(dsts[2 * t], keys[2 * t // 7][0]) + mm(dsts[2 * t + 1], keys[(2 * t + 1) // 7][1])
        dq_tiles.append((total * cosine - swapped(total) * sine).astype(BF16))
    dq = jnp.concatenate(dq_tiles, axis=1)
    grad(QUERY, mm_tn(a_pad, dq))
    part_q = reduce_start(REDUCE[1])
    fg["gg"] = second_axis("gg", fg["gg"])
    da_pad = mm_nt(dq, weight(*QUERY))
    part_q = reduce_0(REDUCE[1], part_q)
    part_o = reduce_1(REDUCE[0], part_o)
    landed(dkv_copy)
    dkv_own = s["dkvf"][yh] + s["dkr"][...].astype(F32)
    dko, dvl = dkv_own[:, 0:128], dkv_own[:, 128:256].astype(BF16)
    dkl = (dko * cosine - swapped(dko) * sine).astype(BF16)
    dkvl = jnp.concatenate([dkl, dvl], axis=1)
    da_pad = da_pad + mm_nt(dkvl, weight(KEY, VALUE))
    hi, lo = split(da_pad)
    dav = mm_nt(hi, pad[...]) + mm_nt(lo, pad[...])
    gain_a_grad = jnp.sum(dav * xf * r1, axis=0, keepdims=True)
    bias_grad = jnp.sum(jnp.concatenate([dq, dkvl], axis=1).astype(F32), axis=0, keepdims=True)
    small = jnp.concatenate([gain_a_grad, gain_f_grad, bias_grad], axis=1)
    spread = (mask[...].astype(F32) * small).astype(BF16)
    small_rows = mm_nt(spread, pick[...]).astype(BF16)
    small_rows = mm_tn(last_rows, jnp.concatenate([small_rows, jnp.zeros((128, 96), BF16)], axis=1))
    kv_grad = mm_tn(a_pad, dkvl)
    grad((KEY,), kv_grad[:, 0:128] + small_rows)
    grad((VALUE,), kv_grad[:, 128:256])
    part_k = reduce_start(REDUCE[2])

    fv = dav * gain_a
    inner = jnp.mean(fv * xf, axis=-1, keepdims=True)
    store("ing", (dh + r1 * fv - xf * (r1 * r1 * r1 * inner)).astype(BF16))

    part_k = reduce_0(REDUCE[2], part_k)
    fg["gu"] = second_axis("gu", fg["gu"])
    part_q = reduce_1(REDUCE[1], part_q)
    part_o = reduce_2(REDUCE[0], part_o)
    for t, total in reduce_sum(REDUCE[2], "gat", "r1", 0, part_k):
        s["t2"][t] = total.astype(BF16)
    part_k = group("tile")
    for n, (i, j) in enumerate(plane):
        remote(s["t2"].at[4, (x + i) % 4, (z + j) % 4], s["rp"].at[n], device((x + i) % 4, y, (z + j) % 4, c), part_k, 1)
    chunk_copies(2)[3].start()
    red_o[2][2] = 1
    s["wf"][0] = owned("gg", fg["gg"])
    s["wf"][1] = owned("gu", fg["gu"])
    for at in range(8):
        rows = []
        for g in range(2):
            rows += [s["wf"][g, 7 * at:7 * at + 7], jnp.zeros((1, FS), F32)]
        s["fs"][at] = jnp.concatenate(rows, axis=0).astype(BF16)
    fin_in = group("piece")
    for k in range(4):
        for e in range(2):
            if k or e:
                ty, tc = (y + k) % 4, (c + e) % 2
                remote(s["fs"].at[ty * 2 + tc], s["fr"].at[me8], device(x, ty, z, tc), fin_in, 1)
    s["fr"][me8] = s["fs"][me8]
    part_q = reduce_2(REDUCE[1], part_q)
    store("g_down", jnp.concatenate([owned("ga", fg["ga"])[0:38], owned("gb", fg["gb"])[0:38]], axis=1))
    landed(*red_o[1:])
    total = hidden + s["po"][y, c].astype(F32)
    for k in range(3):
        total = total + s["ro"][k].astype(F32)
    store("out", total.astype(BF16))
    landed(fin_in)
    for yy in range(2):
        for xx in range(4):
            block = jnp.zeros((16, FS), F32)
            lane16 = iota((16, FS), 1)
            for q in range(4):
                moved = s["fr"][(2 * (q % 2) + yy) * 2 + q // 2].astype(F32)
                if xx != q:
                    moved = pltpu.roll(moved, (160 * (q - xx)) % FS, 1)
                block = jnp.where((lane16 >= 160 * q) & (lane16 < 160 * q + 160), moved, block)
            guf[:, 2 * xx + yy] = block.reshape(2, 8, FS)
    hi, lo = split(guf[...].reshape(128, FS))
    flat = (mm_nt(hi, order[...]) + mm_nt(lo, order[...])).reshape(2, 8, 8, FS)
    for g, name in enumerate(("g_gate", "g_up")):
        for k in range(8):
            o_[name][:, 608 * k:608 * k + 608] = flat[g, k, 0:7, 0:608]
        stores[name].start()

    reduce_3(REDUCE[0], part_o)
    reduce_3(REDUCE[1], part_q)
    landed(part_k)
    total = s["t2"][4, x, z].astype(F32)
    for n in range(15):
        total = total + s["rp"][n].astype(F32)
    s["fin"][4] = total
    fin_copy = group("fin")
    remote(s["fin"].at[:, pl.ds((1 - c) * 8, 8)], s["finr"], sibling, fin_copy, 8)
    landed(fin_copy)
    for t in range(8):
        own = jnp.where(c == 0, s["fin"][t, 0:8], s["fin"][t, 8:16])
        other = s["finr"][t]
        pkf[:, LANES[t]:LANES[t] + 128] = jnp.where(c == 0, own, other)
        pkf[:, LANES[8 + t]:LANES[8 + t] + 128] = jnp.where(c == 0, other, own)
    store("g_wq", pkf[0:7, 0:896])
    store("g_wk", pkf[0:7, 896:1024])
    store("g_wv", pkf[0:7, 1024:1152])
    store("g_wo", pkf[0:7, 1152:2048])
    store("g_gain_attn", pkf[7:8, 896:903])
    store("g_gain_ffn", pkf[7:8, 903:910])
    store("g_bias", pkf[7:8, 910:919])
    for k in range(4):
        chunk_copies(k)[0].wait_send()
        for name in ("ball", "yall"):
            passing(name, k).wait_send()
            if k:
                arriving(name, k).wait_send()
    for to in groups:
        if to[2]:
            wait_for(ssem, to)
    for copy in stores.values():
        copy.wait()
    assert count[0] <= NSEM, count[0]


def hand_over(*refs):
    n = len(OUTPUTS)
    copies = [pltpu.make_async_copy(refs[k], refs[n + k], refs[2 * n].at[k]) for k in range(n)]
    for copy in copies:
        copy.start()
    for copy in copies:
        copy.wait()


def per_device(*args):
    shapes = tuple(jax.ShapeDtypeStruct(*v) for v in OUTPUTS.values())
    anywhere = pl.BlockSpec(memory_space=pl.ANY)
    results = pl.pallas_call(
        body,
        out_shape=shapes,
        in_specs=[anywhere] * len(INPUTS),
        out_specs=(anywhere,) * len(OUTPUTS),
        scratch_shapes=[
            pltpu.VMEM(shape, dtype) for part in (SCRATCH, INPUTS, OUTPUTS) for shape, dtype in part.values()]
        + [pltpu.SemaphoreType.DMA((n,)) for n in (NSEM, NSEM, len(INPUTS), len(OUTPUTS))],
        compiler_params=pltpu.CompilerParams(
            collective_id=0, has_side_effects=True, vmem_limit_bytes=60 * 2**20),
        name="layer",
    )(*(v.reshape(1, -1) if v.ndim == 1 else v for v in args))
    results = pl.pallas_call(
        hand_over,
        out_shape=shapes,
        in_specs=[anywhere] * len(OUTPUTS),
        out_specs=(pl.BlockSpec(memory_space=pltpu.VMEM),) * len(OUTPUTS),
        scratch_shapes=[pltpu.SemaphoreType.DMA((len(OUTPUTS),))],
        name="results",
    )(*results)
    return tuple(v.reshape(-1) if v.shape[0] == 1 else v for v in results)


def solution(mesh):
    both = P(("dp", "ctx"))
    rows = P(("dp", "ctx"), None)
    return jax.shard_map(
        per_device,
        mesh=mesh,
        in_specs=(rows, both, both, rows, rows, rows, both, rows, both, rows, rows, rows, rows),
        out_specs=(rows, rows, both, rows, rows, rows, both, rows, both, rows, rows, rows),
        check_vma=False,
    )
```
